128 devices in a mesh: side: 2 (over core), row: 8 (over z_hi, y), col: 8 (over z_lo, x).
Axes of the slice: x: 4, y: 4, z: 4 (z_hi: 2, z_lo: 2; z = z_hi * 2 + z_lo), core: 2. Of those that a mesh axis runs over, the one named last changes fastest.
Arguments:
- queries: bfloat16 [1024, 128, 576], P(('side', 'row'), 'col'), may hold values from -48 to 48
- cache: bfloat16 [1024, 128, 576], P(('side', 'row')), may hold values from -4 to 4
- lengths: int32 [1024], P(('side', 'row')), may hold values from 2 to 128, as said below
- w_uv: bfloat16 [128, 512, 128], P('col'), may hold values from -0.25 to 0.25
- w_out: bfloat16 [16384, 7168], P('col', ('side', 'row')), may hold values from -0.046875 to 0.046875
- residual_in: bfloat16 [1024, 7168], P('col', ('side', 'row')), may hold values from -8 to 8
- norm_gain: bfloat16 [7168], P(('side', 'row')), may hold values from 0.099609375 to 1.8984375
- expert_ids: int32 [1024, 8], P('col'), may hold values from 0 to 15, all different within a row; in each aligned block of 128 rows (0 to 127, 128 to 255, ...) at most 96 rows name the same one
- gate_vals: float32 [1024, 8], P('col'), may hold values from 0.05 to 0.5
- w_gate: bfloat16 [16, 7168, 2048], P(('side', 'row'), None, 'col'), may hold values from -0.0625 to 0.0625
- w_up: bfloat16 [16, 7168, 2048], P(('side', 'row'), None, 'col'), may hold values from -0.0625 to 0.0625
- w_down: bfloat16 [16, 2048, 7168], P(('side', 'row'), 'col'), may hold values from -0.125 to 0.125
Outputs:
- mixed: bfloat16 [1024, 7168], P('col', ('side', 'row'))
The draws below stay inside these ranges and needn't reach their ends.
Inputs may be any that keep to these rules, and one draw needn't show every extreme that they name: Row b's cache holds its keys in slots below lengths[b]; some row has all 128 slots live. `expert_ids`: each row names 8 different experts; within each aligned block of 128 rows no expert is named by more than 96 rows.
All inputs are finite; a program needn't handle non-finite values.
Results may differ from the reference program's by a relative error of at most 0.015.
Values may be sent and summed in bfloat16 or wider, within the bound.
A program may use at most 192 MiB of HBM per device.

```python
import math
import jax
import jax.numpy as jnp
import numpy as np
from jax import lax

D = 7168
H = 128
KVL = 512
ROPE = 64
HD = 128
FF = 2048
L = 128
LAT = 576
EXPERTS = 16
TOP = 8
TOKENS = 1024
BLOCK = 128
CAPACITY = 96
N_COL = 8


def cache_values(key):
    return jax.random.truncated_normal(key, -4.0, 4.0, (TOKENS, L, LAT), jnp.float32)


def draw_cache(key, part):
    return cache_values(key).astype(jnp.bfloat16)


def draw_queries(key, part):
    key = jax.random.fold_in(key, 11)
    values = jax.random.truncated_normal(key, -4.0, 4.0, (TOKENS, H, LAT), jnp.float32)
    return values.astype(jnp.bfloat16)


def draw_lengths(key, part):
    key = jax.random.fold_in(key, 5)
    values = jax.random.randint(key, (TOKENS,), 2, L + 1)
    first_row = jnp.arange(TOKENS) == 0
    return jnp.where(first_row, L, values).astype(jnp.int32)


def draw_residual_in(key, part):
    key = jax.random.fold_in(key, 7)
    column_pos = jnp.arange(D, dtype=jnp.float32) / D
    column_scale = jnp.exp(jnp.log(0.4) + jnp.log(5.0) * column_pos)
    values = jax.random.truncated_normal(key, -4.0, 4.0, (TOKENS, D), jnp.float32) * column_scale
    return values.astype(jnp.bfloat16)


def block_levels(own_key, shape, split, low, largest):
    factor_of, own = 1.0, jax.random.fold_in(own_key, 6)
    for dim, shards_of in split:
        draws = jnp.exp(jax.random.uniform(jax.random.fold_in(own, dim), (shards_of,), jnp.float32, low / len(split), largest / len(split)))
        factor_of = factor_of * jnp.repeat(draws, shape[dim] // shards_of).reshape([-1 if axis == dim else 1 for axis in range(len(shape))])
    return factor_of


def deal_out(stream_key, own, number, rows, count, top, reach, skew):
    order = jax.random.permutation(stream_key, count)
    crowded, common = load_shares(count, rows * top, reach, skew, True), load_shares(count, rows * top, reach, skew, False)
    places = jnp.arange(count)

    def named(tallies, turn):
        used = int((tallies > 0).sum())
        fixed = max(1, used // 4)
        shifted = fixed + (places - fixed + turn * (used - fixed)) % max(1, count - fixed)
        return jnp.zeros((count,), jnp.int32).at[order[jnp.where(places < fixed, places, shifted)]].set(jnp.asarray(tallies, jnp.int32))

    tallies = jnp.where(number % 4 == 0, named(crowded, number // 4), named(common, number - number // 4 - 1))
    mixed = jax.random.permutation(jax.random.fold_in(own, 3), count)
    giver, receiver = mixed[0:count // 2 * 2:2], mixed[1:count // 2 * 2:2]
    slack = jnp.minimum(tallies[giver] - 1, reach - tallies[receiver]) // 2
    slack = jnp.where((giver == order[0]) | (receiver == order[0]) | (tallies[receiver] == 0), 0, jnp.maximum(slack, 0))
    shifted = jax.random.randint(jax.random.fold_in(own, 4), (count // 2,), 0, 1 << 20) % (slack + 1)
    tallies = tallies.at[giver].add(-shifted).at[receiver].add(shifted)
    labels = jnp.searchsorted(jnp.cumsum(tallies), jnp.arange(rows * top), side="right").astype(jnp.int32)
    listing = labels.reshape(top, rows).T
    listing = listing[jax.random.permutation(jax.random.fold_in(own, 1), rows)]
    turn = jax.random.randint(jax.random.fold_in(own, 2), (rows, 1), 0, top)
    return jnp.take_along_axis(listing, (jnp.arange(top)[None, :] + turn) % top, axis=1)


def load_shares(count, total, limit, slope, full):
    loads = [(1 << 20) // math.isqrt(rank ** slope) + 1 for rank in range(1, count + 1)]
    largest = limit if full else min(limit, max(-(-total // count), total * loads[0] // sum(loads)))
    least = 1 if total - largest >= count - 1 else 0
    holding, spare = [largest] + [least] * (count - 1), total - largest - least * (count - 1)
    while spare > 0:
        movable = [i for i in range(1, count) if holding[i] < largest] or [i for i in range(1, count) if holding[i] < limit]
        pool, budget = sum([loads[i] for i in movable]), spare
        for i in movable:
            extra = min(limit - holding[i], max(1, budget * loads[i] // pool), spare)
            holding[i] = holding[i] + extra
            spare = spare - extra
    return np.array(holding)


def bell_draw(own_key, extent, deviation, limit, cuts=(), held_as=jnp.bfloat16):
    drawn = jax.random.normal(own_key, extent, jnp.float32) * deviation
    if len(cuts) > 0:
        drawn = block_levels(own_key, extent, cuts, -0.22, 0.18) * drawn
    return jnp.clip(drawn, min=-limit, max=limit).astype(held_as)


def setup_inputs(seed: int = 0) -> dict:
    arg_keys = jax.random.split(jax.random.key(seed), 13)
    queries = draw_queries(jax.random.fold_in(arg_keys[12], 71), 0)
    cache = draw_cache(jax.random.fold_in(arg_keys[12], 71), 0)
    lengths = draw_lengths(jax.random.fold_in(arg_keys[12], 71), 0)
    w_uv = bell_draw(arg_keys[3], (H, KVL, HD), KVL ** -0.5, 0.25, ((0, 8),))
    w_out = bell_draw(arg_keys[4], (H * HD, D), (H * HD) ** -0.5, 0.046875, ((0, 8), (1, 16)))
    residual_in = draw_residual_in(jax.random.fold_in(arg_keys[12], 71), 0)
    norm_gain = jnp.clip(1.0 + 0.18 * jax.random.normal(arg_keys[6], (D,), jnp.float32), 0.099609375, 1.8984375).astype(jnp.bfloat16)
    expert_ids_keys = jax.random.split(jax.random.fold_in(arg_keys[7], 1), TOKENS // BLOCK)
    expert_ids_turns = jax.random.permutation(jax.random.fold_in(arg_keys[7], 3), TOKENS // BLOCK)
    expert_ids = jax.vmap(lambda own, number: deal_out(jax.random.fold_in(arg_keys[7], 2), own, number, BLOCK, EXPERTS, TOP, CAPACITY, 1))(expert_ids_keys, expert_ids_turns).reshape((TOKENS, TOP))
    gate_vals = jnp.clip(jnp.exp(math.log(0.5) - 2.3025851 * jax.random.uniform(arg_keys[8], (TOKENS, TOP), jnp.float32) ** block_levels(arg_keys[8], (TOKENS, TOP), ((0, 8),), -0.2, 0.2)), 0.05, 0.5)
    w_gate = bell_draw(arg_keys[9], (EXPERTS, D, FF), D ** -0.5, 0.0625, ((0, 16), (2, 8)))
    w_up = bell_draw(arg_keys[10], (EXPERTS, D, FF), D ** -0.5, 0.0625, ((0, 16), (2, 8)))
    w_down = bell_draw(arg_keys[11], (EXPERTS, FF, D), FF ** -0.5, 0.125, ((0, 16), (1, 8)))
    return dict(queries=queries, cache=cache, lengths=lengths, w_uv=w_uv, w_out=w_out, residual_in=residual_in, norm_gain=norm_gain, expert_ids=expert_ids, gate_vals=gate_vals, w_gate=w_gate, w_up=w_up, w_down=w_down)


def reference(queries, cache, lengths, w_uv, w_out, residual_in, norm_gain, expert_ids, gate_vals, w_gate, w_up, w_down):
    score_scale = (HD + ROPE) ** (-0.5)
    query_wide = queries.astype(jnp.float32)
    cache_wide = cache.astype(jnp.float32)
    scores = jnp.einsum('bhk,blk->bhl', query_wide, cache_wide) * score_scale
    places = jnp.arange(L, dtype=jnp.int32)
    live_mask = places[None, None, :] < lengths[:, None, None]
    scores = jnp.where(live_mask, scores, -jnp.inf)
    row_top = lax.optimization_barrier(jnp.max(scores, axis=2, keepdims=True))
    exp_terms = jnp.exp(scores - row_top)
    attn_probs = (exp_terms / lax.optimization_barrier(jnp.sum(exp_terms, axis=2, keepdims=True))).astype(jnp.bfloat16)
    latent = jnp.einsum('bhl,blk->bhk', attn_probs.astype(jnp.float32), cache_wide[:, :, :KVL]).astype(jnp.bfloat16)
    head_out = jnp.einsum('bhk,hkd->bhd', latent.astype(jnp.float32), w_uv.astype(jnp.float32)).astype(jnp.bfloat16)
    head_out = head_out.reshape(TOKENS, H * HD)
    attention = jnp.dot(head_out, w_out, preferred_element_type=jnp.float32)
    hidden = residual_in.astype(jnp.float32) + attention
    inverse = lax.rsqrt(lax.optimization_barrier(jnp.sum(hidden * hidden, axis=1, keepdims=True)) / D + 1e-06)
    normed = (hidden * inverse * norm_gain.astype(jnp.float32)).astype(jnp.bfloat16)
    part_width = FF // N_COL

    def one_expert(running, items):
        expert_index, gate_mat, up_mat, down_mat = items
        gate_part = jnp.dot(normed, gate_mat, preferred_element_type=jnp.float32)
        up_part = jnp.dot(normed, up_mat, preferred_element_type=jnp.float32)
        activation = (jax.nn.silu(gate_part) * up_part).astype(jnp.bfloat16)
        pieces = jnp.einsum('bpw,pwd->pbd', activation.astype(jnp.float32).reshape(TOKENS, N_COL, part_width), down_mat.astype(jnp.float32).reshape(N_COL, part_width, D))
        rounded = lax.optimization_barrier(pieces.astype(jnp.bfloat16)).astype(jnp.float32)
        expert_rows = lax.optimization_barrier(jnp.sum(rounded, axis=0))
        weight_row = lax.optimization_barrier(jnp.sum(jnp.where(expert_ids == expert_index, gate_vals, 0.0), axis=1))
        return (running + weight_row[:, None] * expert_rows, None)
    start_total = jnp.zeros((TOKENS, D), jnp.float32)
    expert_total, unused = lax.scan(one_expert, start_total, (jnp.arange(EXPERTS, dtype=jnp.int32), w_gate, w_up, w_down))
    return (hidden + expert_total).astype(jnp.bfloat16)
```

```python
import functools

import jax
import jax.numpy as jnp
from jax import lax
from jax.experimental import pallas as pl
from jax.experimental.pallas import tpu as pltpu
from jax.sharding import PartitionSpec as P

D = 7168
ROPE = 64
HD = 128
HALF = 64
PAIR = 896
MESH = pl.DeviceIdType.MESH
BF16 = jnp.bfloat16
F32 = jnp.float32

LANES = ((0, 384), (384, 256), (640, 256))
ORDERS = (("x", "y", "z"), ("y", "z", "x"), ("z", "x", "y"))
SIZES = {"x": (2, 2, 4), "y": (2, 4, 2), "z": (4, 4)}


def position():
    row, col = lax.axis_index("row"), lax.axis_index("col")
    return {"x": col % 4, "y": row % 4, "z": (row // 4) * 2 + col // 4}


def chip_id(at):
    return (lax.axis_index("side"), (at["z"] // 2) * 4 + at["y"], (at["z"] % 2) * 4 + at["x"])


def neighbour(here, axis, step):
    return chip_id({**here, axis: (here[axis] + step + 4) % 4})


def sibling_id():
    return (1 - lax.axis_index("side"), lax.axis_index("row"), lax.axis_index("col"))


def view(ref, at, rows, lanes, lead=()):
    index = [slice(None)] * 4
    if "x" in at:
        index[1] = at["x"]
    if "y" in at:
        index[3] = at["y"]
    if "z" in at:
        index[0], index[2] = at["z"] % 2, at["z"] // 2
    return ref.at[(*lead, *index, pl.ds(*rows), pl.ds(*lanes))]


def lead_shape(fixed):
    shape = []
    if "z" not in fixed:
        shape.append(2)
    if "x" not in fixed:
        shape.append(4)
    if "z" not in fixed:
        shape.append(2)
    if "y" not in fixed:
        shape.append(4)
    return tuple(shape)


def enter(peers):
    barrier = pltpu.get_barrier_semaphore()
    for peer in peers:
        pl.semaphore_signal(barrier, inc=1, device_id=peer, device_id_type=MESH)
    pl.semaphore_wait(barrier, len(peers))


def ring_peers(here):
    return [sibling_id()] + [neighbour(here, axis, step) for axis in "xyz" for step in (1, -1)]


LOW, HIGH, ALL = (0, 32), (32, 32), (0, 64)


def gather_kernel(
    hidden_ref, gain_ref, gates_ref, gate_hbm, up_hbm, act_ref,
    rows_buf, weights, squares, total, load_sem, sq_send, sq_recv, send_sem, recv_sem, sib_send, sib_recv,
):
    side = lax.axis_index("side")
    row = lax.axis_index("row")
    here = position()
    loads = []
    for which, source in enumerate((gate_hbm, up_hbm)):
        for core in range(2):
            loads.append(
                pltpu.make_async_copy(
                    source.at[core],
                    weights.at[:, core, :, pl.ds(which * 256, 256)],
                    load_sem.at[which * 2 + core],
                )
            )
    for load in loads:
        load.start()
    row_peers = []
    for k in range(1, 8):
        other = (row + k) % 8
        row_peers.append((side, other, lax.axis_index("col")))
    enter(ring_peers(here) + row_peers)

    hidden = hidden_ref[...]
    squares[row] = jnp.broadcast_to(jnp.sum(hidden * hidden, axis=1, keepdims=True), (HALF, 128))
    copies = []
    for k in range(1, 8):
        copy = pltpu.make_async_remote_copy(
            src_ref=squares.at[row],
            dst_ref=squares.at[row],
            send_sem=sq_send.at[k],
            recv_sem=sq_recv.at[k],
            device_id=row_peers[k - 1],
            device_id_type=MESH,
        )
        copy.start()
        copies.append(copy)
    for copy in copies:
        copy.wait()
    sums = squares[0]
    for k in range(1, 8):
        sums = sums + squares[k]
    inverse = lax.rsqrt(sums[:, :1] / D + 1e-06)
    rows_buf[side, here["z"] % 2, here["x"], here["z"] // 2, here["y"]] = (
        hidden * inverse * gain_ref[...]
    ).astype(BF16)

    def ring_copy(part, phase, direction, piece, at, rows):
        axis = ORDERS[part][phase]
        ref = view(rows_buf, at, rows, LANES[part], (side,))
        return pltpu.make_async_remote_copy(
            src_ref=ref,
            dst_ref=ref,
            send_sem=send_sem.at[part, phase, direction, piece],
            recv_sem=recv_sem.at[part, phase, direction, piece],
            device_id=neighbour(here, axis, 1 - 2 * direction),
            device_id_type=MESH,
        )

    def share(part, index, at):
        ref = view(rows_buf, at, ALL, LANES[part], (side,))
        return pltpu.make_async_remote_copy(
            src_ref=ref,
            dst_ref=ref,
            send_sem=sib_send.at[part, index],
            recv_sem=sib_recv.at[part, index],
            device_id=sibling_id(),
            device_id_type=MESH,
        )

    sent, shared = [], []
    for phase in range(3):
        started = {}
        for part in range(3):
            axis = ORDERS[part][phase]
            own = {a: here[a] for a in ORDERS[part][phase:]}
            for direction, halves in enumerate(((LOW, HIGH), (HIGH, LOW))):
                for piece in range(2):
                    copy = ring_copy(part, phase, direction, piece, own, halves[piece])
                    copy.start()
                    started[part, direction, piece] = copy
            if phase == 2:
                copy = share(part, 0, own)
                copy.start()
                shared.append(copy)
        for part in range(3):
            axis = ORDERS[part][phase]
            own = {a: here[a] for a in ORDERS[part][phase:]}
            for direction, half in enumerate((LOW, HIGH)):
                step = 1 - 2 * direction
                started[part, direction, 0].wait_recv()
                source = {**own, axis: (here[axis] - step + 4) % 4}
                copy = ring_copy(part, phase, direction, 2, source, half)
                copy.start()
                started[part, direction, 2] = copy
        for part in range(3):
            axis = ORDERS[part][phase]
            own = {a: here[a] for a in ORDERS[part][phase:]}
            for direction in range(2):
                step = 1 - 2 * direction
                started[part, direction, 1].wait_recv()
                if phase == 2:
                    copy = share(part, 1 + direction, {**own, axis: (here[axis] - step + 4) % 4})
                    copy.start()
                    shared.append(copy)
        for part in range(3):
            axis = ORDERS[part][phase]
            own = {a: here[a] for a in ORDERS[part][phase:]}
            for direction in range(2):
                started[part, direction, 2].wait_recv()
            if phase == 2:
                copy = share(part, 3, {**own, axis: (here[axis] + 2) % 4})
                copy.start()
                shared.append(copy)
        sent += list(started.values())

    for load in loads:
        load.wait()

    def experts(half):
        total[...] = jnp.zeros_like(total)

        @pl.loop(0, 8)
        def _(r):
            lhs = rows_buf[half, :, :, r // 4, r % 4].reshape(8 * HALF, PAIR)
            total[...] += jnp.dot(lhs, weights[r].reshape(PAIR, 512), preferred_element_type=F32)

        gate_part = total[:, :256]
        value = gate_part / (1.0 + jnp.exp(-gate_part)) * total[:, 256:]
        act_ref[half] = (value * gates_ref[half]).astype(BF16)

    experts(side)
    for copy in shared:
        copy.wait_recv()
    experts(1 - side)
    for copy in sent + shared:
        copy.wait_send()


def scatter_kernel(
    act_ref, down_ref, hidden_ref, out_ref,
    stage, from_sibling, sums, mixed, mixed_sibling, *rest,
):
    arrivals, (sib_send, sib_recv, send_sem, recv_sem, out_send, out_recv) = rest[:9], rest[9:]
    side = lax.axis_index("side")
    here = position()
    enter(ring_peers(here))

    def sibling_copy(r):
        return pltpu.make_async_remote_copy(
            src_ref=stage.at[r],
            dst_ref=from_sibling.at[r],
            send_sem=sib_send.at[r],
            recv_sem=sib_recv.at[r],
            device_id=sibling_id(),
            device_id_type=MESH,
        )

    @pl.loop(0, 8)
    def _(r):
        stage[r] = jnp.dot(act_ref[1 - side], down_ref[r], preferred_element_type=F32).astype(BF16)
        sibling_copy(r).start()

    @pl.loop(0, 8)
    def _(r):
        own = jnp.dot(act_ref[side], down_ref[r], preferred_element_type=F32)
        sibling_copy(r).wait_recv()
        both = own + from_sibling[r].astype(F32)
        sums[:, :, r // 4, r % 4] = both.astype(BF16).reshape(2, 4, HALF, PAIR)

    def ring_copy(part, phase, direction, piece, at, rows):
        axis = ORDERS[part][phase]
        return pltpu.make_async_remote_copy(
            src_ref=view(sums, at, rows, LANES[part]),
            dst_ref=arrivals[part * 3 + phase].at[direction, piece],
            send_sem=send_sem.at[part, phase, direction, piece],
            recv_sem=recv_sem.at[part, phase, direction, piece],
            device_id=neighbour(here, axis, 1 - 2 * direction),
            device_id_type=MESH,
        )

    sent = []
    for phase in range(3):
        started = {}
        for part in range(3):
            axis = ORDERS[part][phase]
            done = {a: here[a] for a in ORDERS[part][:phase]}
            far = {**done, axis: (here[axis] + 2) % 4}
            for direction, (through, direct) in enumerate(((LOW, HIGH), (HIGH, LOW))):
                step = 1 - 2 * direction
                near = {**done, axis: (here[axis] + step + 4) % 4}
                for piece, (at, rows) in enumerate(((far, through), (near, direct))):
                    copy = ring_copy(part, phase, direction, piece, at, rows)
                    copy.start()
                    started[part, direction, piece] = copy
        for part in range(3):
            axis = ORDERS[part][phase]
            done = {a: here[a] for a in ORDERS[part][:phase]}
            arrived = arrivals[part * 3 + phase]
            for direction, through in enumerate((LOW, HIGH)):
                step = 1 - 2 * direction
                near = {**done, axis: (here[axis] + step + 4) % 4}
                started[part, direction, 0].wait_recv()
                target = view(sums, near, through, LANES[part])
                target[...] = (target[...].astype(F32) + arrived[direction, 0].astype(F32)).astype(BF16)
                copy = ring_copy(part, phase, direction, 2, near, through)
                copy.start()
                started[part, direction, 2] = copy
        for part in range(3):
            axis = ORDERS[part][phase]
            own = {a: here[a] for a in ORDERS[part][: phase + 1]}
            arrived = arrivals[part * 3 + phase]
            for direction in range(2):
                started[part, direction, 1].wait_recv()
                started[part, direction, 2].wait_recv()
            for rows, (first, second) in ((LOW, (2, 1)), (HIGH, (1, 2))):
                target = view(sums, own, rows, LANES[part])
                value = target[...].astype(F32) + (
                    arrived[0, first].astype(F32) + arrived[1, second].astype(F32)
                )
                if phase < 2:
                    target[...] = value.astype(BF16)
                else:
                    spot = (pl.ds(*rows), pl.ds(*LANES[part]))
                    mixed[spot] = (hidden_ref[spot] + value).astype(BF16)
        sent += list(started.values())

    copy = pltpu.make_async_remote_copy(
        src_ref=mixed,
        dst_ref=mixed_sibling,
        send_sem=out_send,
        recv_sem=out_recv,
        device_id=sibling_id(),
        device_id_type=MESH,
    )
    copy.start()
    copy.wait_recv()

    @pl.when(side == 0)
    def _():
        out_ref[0:64] = mixed[:, 0:448]
        out_ref[64:128] = mixed_sibling[:, 0:448]

    @pl.when(side == 1)
    def _():
        out_ref[0:64] = mixed_sibling[:, 448:896]
        out_ref[64:128] = mixed[:, 448:896]

    copy.wait_send()
    for copy in sent:
        copy.wait_send()

    @pl.loop(0, 8)
    def _(r):
        sibling_copy(r).wait_send()


VMEM = pl.BlockSpec(memory_space=pltpu.VMEM)
ANY = pl.BlockSpec(memory_space=pl.ANY)


def gather_call(hidden, gain, gates, w_gate, w_up):
    return pl.pallas_call(
        gather_kernel,
        out_shape=jax.ShapeDtypeStruct((2, 8 * HALF, 256), BF16),
        in_specs=[VMEM, VMEM, VMEM, ANY, ANY],
        out_specs=VMEM,
        scratch_shapes=[
            pltpu.VMEM((2, 2, 4, 2, 4, HALF, PAIR), BF16),
            pltpu.VMEM((8, 2, 448, 512), BF16),
            pltpu.VMEM((8, HALF, 128), F32),
            pltpu.VMEM((8 * HALF, 512), F32),
            pltpu.SemaphoreType.DMA((4,)),
            pltpu.SemaphoreType.DMA((8,)),
            pltpu.SemaphoreType.DMA((8,)),
            pltpu.SemaphoreType.DMA((3, 3, 2, 3)),
            pltpu.SemaphoreType.DMA((3, 3, 2, 3)),
            pltpu.SemaphoreType.DMA((3, 4)),
            pltpu.SemaphoreType.DMA((3, 4)),
        ],
        compiler_params=pltpu.CompilerParams(
            collective_id=0, has_side_effects=True, vmem_limit_bytes=48 * 2**20
        ),
        cost_estimate=pl.CostEstimate(
            flops=2 * 1024 * 7168 * 512, bytes_accessed=8 * 2**20, transcendentals=2**18
        ),
    )(hidden, gain, gates, w_gate, w_up)


def scatter_call(act, down, hidden):
    arrivals = []
    for part in range(3):
        for phase in range(3):
            fixed = ORDERS[part][: phase + 1]
            arrivals.append(pltpu.VMEM((2, 3, *lead_shape(fixed), 32, LANES[part][1]), BF16))
    return pl.pallas_call(
        scatter_kernel,
        out_shape=jax.ShapeDtypeStruct((2 * HALF, 448), BF16),
        in_specs=[VMEM, VMEM, VMEM],
        out_specs=VMEM,
        scratch_shapes=[
            pltpu.VMEM((8, 8 * HALF, PAIR), BF16),
            pltpu.VMEM((8, 8 * HALF, PAIR), BF16),
            pltpu.VMEM((2, 4, 2, 4, HALF, PAIR), BF16),
            pltpu.VMEM((HALF, PAIR), BF16),
            pltpu.VMEM((HALF, PAIR), BF16),
            *arrivals,
            pltpu.SemaphoreType.DMA((8,)),
            pltpu.SemaphoreType.DMA((8,)),
            pltpu.SemaphoreType.DMA((3, 3, 2, 3)),
            pltpu.SemaphoreType.DMA((3, 3, 2, 3)),
            pltpu.SemaphoreType.DMA,
            pltpu.SemaphoreType.DMA,
        ],
        compiler_params=pltpu.CompilerParams(
            collective_id=1, has_side_effects=True, vmem_limit_bytes=52 * 2**20
        ),
        cost_estimate=pl.CostEstimate(
            flops=2 * 1024 * 7168 * 256, bytes_accessed=4 * 2**20, transcendentals=0
        ),
    )(act, down, hidden)


def shards(
    queries,
    cache,
    lengths,
    w_uv,
    w_out,
    residual_in,
    norm_gain,
    expert_ids,
    gate_vals,
    w_gate,
    w_up,
    w_down,
):
    side = lax.axis_index("side")
    owner_index = lax.axis_index(("side", "row"))
    my_gate = jnp.sum(jnp.where(expert_ids == owner_index, gate_vals, 0.0), axis=1)
    gates = lax.all_gather(my_gate, "col", axis=0, tiled=True)
    gates = gates.reshape(8, 2, HALF).transpose(1, 0, 2).reshape(2, 8 * HALF, 1)
    pair_out = lax.all_gather(w_out, "side", axis=1, tiled=True)
    pair_residual = lax.all_gather(residual_in, "side", axis=1, tiled=True)
    pair_gain = lax.all_gather(norm_gain, "side", axis=0, tiled=True)

    score_scale = (HD + ROPE) ** (-0.5)
    scores = (
        jnp.einsum("rhk,rlk->rhl", queries, cache, preferred_element_type=jnp.float32) * score_scale
    )
    places = lax.broadcasted_iota(jnp.int32, (1, 1, cache.shape[1]), 2)
    scores = jnp.where(places < lengths[:, None, None], scores, -jnp.inf)
    row_top = jnp.max(scores, axis=2, keepdims=True)
    exp_terms = jnp.exp(scores - row_top)
    attn_probs = (exp_terms / jnp.sum(exp_terms, axis=2, keepdims=True)).astype(jnp.bfloat16)
    latent_width = w_uv.shape[1]
    latent = jnp.einsum(
        "rhl,rlk->rhk", attn_probs, cache[:, :, :latent_width], preferred_element_type=jnp.float32
    ).astype(jnp.bfloat16)
    head_out = jnp.einsum("rhk,hkd->rhd", latent, w_uv, preferred_element_type=jnp.float32).astype(
        jnp.bfloat16
    )
    head_out = head_out.reshape(head_out.shape[0], -1)
    all_heads = lax.all_gather(head_out, ("side", "row"), axis=0, tiled=True)
    half_heads = lax.dynamic_index_in_dim(all_heads.reshape(8, 2, HALF, -1), side, 1, keepdims=False)
    partial_rows = jnp.dot(half_heads.reshape(8 * HALF, -1), pair_out, preferred_element_type=jnp.float32)
    attn_slice = lax.psum_scatter(
        partial_rows.astype(jnp.bfloat16), "col", scatter_dimension=0, tiled=True
    ).astype(jnp.float32)
    half_residual = lax.dynamic_slice_in_dim(pair_residual, side * HALF, HALF, 0)
    hidden = half_residual.astype(jnp.float32) + attn_slice
    act = gather_call(
        hidden,
        pair_gain.astype(jnp.float32).reshape(1, PAIR),
        gates,
        w_gate.reshape(2, 8, 448, 256),
        w_up.reshape(2, 8, 448, 256),
    )
    down = w_down.reshape(256, 2, 8, 448).transpose(2, 0, 1, 3).reshape(8, 256, PAIR)
    return scatter_call(act, down, hidden)


def solution(mesh):
    placed = (
        P(("side", "row"), "col", None),
        P(("side", "row"), None, None),
        P(("side", "row")),
        P("col", None, None),
        P("col", ("side", "row")),
        P("col", ("side", "row")),
        P(("side", "row")),
        P("col", None),
        P("col", None),
        P(("side", "row"), None, "col"),
        P(("side", "row"), None, "col"),
        P(("side", "row"), "col", None),
    )
    return jax.shard_map(
        shards, mesh=mesh, in_specs=placed, out_specs=P("col", ("side", "row")), check_vma=False
    )
```

```python
import jax
import jax.numpy as jnp
from jax import lax
from jax.experimental import pallas as pl
from jax.experimental.pallas import tpu as pltpu
from jax.sharding import PartitionSpec as P

D = 7168
ROPE = 64
HD = 128
HALF = 64
OWN = 448
PAIR = 896
MESH = pl.DeviceIdType.MESH
BF16 = jnp.bfloat16
F32 = jnp.float32

LANES = ((0, 384), (384, 256), (640, 256))
ORDERS = (
    (("x", "y", "z"), ("y", "z", "x"), ("z", "x", "y")),
    (("y", "z", "x"), ("z", "x", "y"), ("x", "y", "z")),
)
HEAD_LANES = ((0, 1152), (1152, 896))
SUM_LANES = ((0, 512), (512, 384))
LOW, HIGH, ALL = (0, 32), (32, 32), (0, 64)


def position():
    row, col = lax.axis_index("row"), lax.axis_index("col")
    return {"x": col % 4, "y": row % 4, "z": (row // 4) * 2 + col // 4}


def chip_id(at):
    return (lax.axis_index("side"), (at["z"] // 2) * 4 + at["y"], (at["z"] % 2) * 4 + at["x"])


def neighbour(here, axis, step):
    return chip_id({**here, axis: (here[axis] + step + 4) % 4})


def sibling_id():
    return (1 - lax.axis_index("side"), lax.axis_index("row"), lax.axis_index("col"))


def view(ref, at, rows, lanes, lead=()):
    index = [slice(None)] * 6
    if "x" in at:
        index[1], index[2] = at["x"] // 2, at["x"] % 2
    if "y" in at:
        index[4], index[5] = at["y"] // 2, at["y"] % 2
    if "z" in at:
        index[0], index[3] = at["z"] % 2, at["z"] // 2
    return ref.at[(*lead, *index, pl.ds(*rows), pl.ds(*lanes))]


def remote(src, dst, send_sem, recv_sem, device):
    return pltpu.make_async_remote_copy(
        src_ref=src,
        dst_ref=dst,
        send_sem=send_sem,
        recv_sem=recv_sem,
        device_id=device,
        device_id_type=MESH,
    )


class RingGather:
    def __init__(self, here, axis, bundle, sems):
        self.here, self.axis, self.bundle, self.sems = here, axis, bundle, sems
        self.copies = {}

    def go(self, direction, piece, j, rows):
        send, recv = self.sems
        ref = self.bundle(j, rows)
        device = neighbour(self.here, self.axis, 1 - 2 * direction)
        copy = remote(ref, ref, send.at[direction, piece], recv.at[direction, piece], device)
        copy.start()
        self.copies[direction, piece] = copy

    def start(self):
        me = self.here[self.axis]
        for piece in range(2):
            for direction, halves in enumerate(((LOW, HIGH), (HIGH, LOW))):
                self.go(direction, piece, me, halves[piece])

    def relay(self):
        for direction, half in enumerate((LOW, HIGH)):
            self.copies[direction, 0].wait_recv()
            self.go(direction, 2, (self.here[self.axis] - 1 + 2 * direction + 4) % 4, half)

    def near(self):
        for direction in range(2):
            self.copies[direction, 1].wait_recv()

    def far(self):
        for direction in range(2):
            self.copies[direction, 2].wait_recv()

    def drain(self):
        for copy in self.copies.values():
            copy.wait_send()


class RingScatter:
    def __init__(self, here, axis, bundle, arrived, sems):
        self.here, self.axis, self.bundle, self.arrived, self.sems = here, axis, bundle, arrived, sems
        self.copies = {}

    def go(self, direction, piece, j, rows):
        send, recv = self.sems
        device = neighbour(self.here, self.axis, 1 - 2 * direction)
        copy = remote(
            self.bundle(j, rows),
            self.arrived.at[direction, piece],
            send.at[direction, piece],
            recv.at[direction, piece],
            device,
        )
        copy.start()
        self.copies[direction, piece] = copy

    def start(self):
        me = self.here[self.axis]
        for direction, half in enumerate((LOW, HIGH)):
            self.go(direction, 0, (me + 2) % 4, half)
        for direction, half in enumerate((HIGH, LOW)):
            self.go(direction, 1, (me + 1 - 2 * direction + 4) % 4, half)

    def relay(self):
        me = self.here[self.axis]
        for direction, half in enumerate((LOW, HIGH)):
            j = (me + 1 - 2 * direction + 4) % 4
            self.copies[direction, 0].wait_recv()
            target = self.bundle(j, half)
            target[...] = (target[...].astype(F32) + self.arrived[direction, 0].astype(F32)).astype(BF16)
            self.go(direction, 2, j, half)

    def finish(self, use=None):
        for direction in range(2):
            self.copies[direction, 1].wait_recv()
            self.copies[direction, 2].wait_recv()
        for rows, (first, second) in ((LOW, (2, 1)), (HIGH, (1, 2))):
            target = self.bundle(self.here[self.axis], rows)
            value = target[...].astype(F32) + (
                self.arrived[0, first].astype(F32) + self.arrived[1, second].astype(F32)
            )
            if use is None:
                target[...] = value.astype(BF16)
            else:
                use(rows, value)

    def drain(self):
        for copy in self.copies.values():
            copy.wait_send()


def layer_kernel(
    head_ref, pair_ref, gate_ref, out_hbm, gate_hbm, up_hbm, down_hbm, out_ref,
    heads, proj, part_sums, z_early, z_late, x_early, x_late, pair_sib, pair_all, hidden,
    rows_buf, weights, down, down_pairs, total, squares, inverses, gates, columns,
    from_sibling, mixed, mixed_sib,
    load_sems, head_sems, flip_sems, sum_sems, pair_sems, proj_sems, small_send, small_recv,
    send_sems, recv_sems, share_send, share_recv, back_send, back_recv, *arrivals,
):
    side, row, col = lax.axis_index("side"), lax.axis_index("row"), lax.axis_index("col")
    here = position()
    x, y, z_hi, z_lo = here["x"], here["y"], here["z"] // 2, here["z"] % 2
    far_z = (side, (row + 4) % 8, col)
    flip_z = (side, row, (col + 4) % 8)
    sibling = sibling_id()
    row_peers = [(side, (row + k) % 8, col) for k in range(1, 8)]
    col_peers = [(side, row, (col + k) % 8) for k in range(1, 8)]

    loads = [
        pltpu.make_async_copy(
            source.at[core],
            weights.at[:, core, :, pl.ds(which * 256, 256)],
            load_sems.at[which * 2 + core],
        )
        for which, source in enumerate((gate_hbm, up_hbm))
        for core in range(2)
    ]
    load_proj = pltpu.make_async_copy(out_hbm, proj.at[side], load_sems.at[4])
    load_down = pltpu.make_async_copy(down_hbm, down, load_sems.at[5])
    load_proj.start()
    for load in loads:
        load.start()
    load_down.start()
    heads[side, z_hi, y // 2, y % 2] = head_ref[...]
    gates[col] = gate_ref[...]

    barrier = pltpu.get_barrier_semaphore()
    peers = [sibling, *row_peers, *col_peers, neighbour(here, "z", 1), neighbour(here, "z", -1)]
    for peer in peers:
        pl.semaphore_signal(barrier, inc=1, device_id=peer, device_id_type=MESH)
    pl.semaphore_wait(barrier, len(peers))

    def head_view(which, at, rows):
        return heads.at[(side, *at, pl.ds(*rows), pl.ds(*HEAD_LANES[which]))]

    def head_sem(which):
        return head_sems.at[0, which], head_sems.at[1, which]

    first = head_view(0, (z_hi, y // 2, y % 2), ALL)
    flip_first = remote(first, first, flip_sems.at[0, 0], flip_sems.at[1, 0], far_z)
    flip_first.start()
    ring_first = RingGather(
        here, "y", lambda j, rows: head_view(1, (z_hi, j // 2, j % 2), rows), head_sem(0)
    )
    ring_first.start()
    pair_copy = remote(pair_ref.at[1 - side], pair_sib, pair_sems.at[0], pair_sems.at[1], sibling)
    pair_copy.start()
    proj_copy = remote(out_hbm, proj.at[side], proj_sems.at[0], proj_sems.at[1], sibling)
    proj_copy.start()
    gate_copies = [
        remote(gates.at[col], gates.at[col], small_send.at[0, k], small_recv.at[0, k], col_peers[k])
        for k in range(7)
    ]
    for copy in gate_copies:
        copy.start()
    flip_first.wait_recv()
    ring_second = RingGather(
        here, "y", lambda j, rows: head_view(0, (slice(None), j // 2, j % 2), rows), head_sem(1)
    )
    ring_second.start()
    ring_first.relay()
    ring_first.near()
    ring_first.far()
    second = head_view(1, (z_hi, slice(None), slice(None)), ALL)
    flip_second = remote(second, second, flip_sems.at[0, 1], flip_sems.at[1, 1], far_z)
    flip_second.start()

    pair_copy.wait_recv()

    @pl.when(side == 0)
    def _():
        pair_all[:, 0:OWN] = pair_ref[0]
        pair_all[:, OWN:PAIR] = pair_sib[...]

    @pl.when(side == 1)
    def _():
        pair_all[:, 0:OWN] = pair_sib[...]
        pair_all[:, OWN:PAIR] = pair_ref[1]

    ring_second.relay()
    ring_second.near()
    ring_second.far()
    flip_second.wait_recv()
    theirs = heads.at[side, :, :, 1 - side]
    head_share = remote(theirs, theirs, pair_sems.at[2], pair_sems.at[3], sibling)
    head_share.start()

    load_proj.wait()
    proj_copy.wait_recv()

    def project(source):
        lhs = heads[source, :, :, side].reshape(4 * HALF, 2048)
        for core in range(2):
            value = jnp.dot(lhs, proj[core], preferred_element_type=F32).astype(BF16)
            part_sums[source, :, :, core * OWN : (core + 1) * OWN] = value.reshape(4, HALF, OWN)

    project(side)
    head_share.wait_recv()
    project(1 - side)

    def sum_sem(which):
        return sum_sems.at[0, which], sum_sems.at[1, which]

    def x_ring(which, lead, arrived):
        return RingScatter(
            here,
            "x",
            lambda j, rows: part_sums.at[lead, j, pl.ds(*rows), pl.ds(*SUM_LANES[which])],
            arrived,
            sum_sem(which),
        )

    early_flip = remote(
        part_sums.at[1 - z_lo, :, :, pl.ds(*SUM_LANES[1])], z_early, flip_sems.at[0, 2], flip_sems.at[1, 2], flip_z
    )
    early_flip.start()
    early_ring = x_ring(0, slice(None), x_early)
    early_ring.start()
    early_ring.relay()
    early_flip.wait_recv()
    mine = part_sums.at[z_lo, :, :, pl.ds(*SUM_LANES[1])]
    mine[...] = (mine[...].astype(F32) + z_early[...].astype(F32)).astype(BF16)
    late_ring = x_ring(1, z_lo, x_late)
    late_ring.start()
    early_ring.finish()
    late_flip = remote(
        part_sums.at[1 - z_lo, x, :, pl.ds(*SUM_LANES[0])], z_late, flip_sems.at[0, 3], flip_sems.at[1, 3], flip_z
    )
    late_flip.start()
    late_ring.relay()
    late_flip.wait_recv()
    left = pl.ds(*SUM_LANES[0])
    hidden[:, left] = pair_all[0:HALF, left].astype(F32) + (
        part_sums[z_lo, x, :, left].astype(F32) + z_late[...].astype(F32)
    )

    def right(rows, value):
        spot = (pl.ds(*rows), pl.ds(*SUM_LANES[1]))
        hidden[spot] = pair_all[spot].astype(F32) + value

    late_ring.finish(right)
    rows_buf[side, z_lo, x // 2, x % 2, z_hi, y // 2, y % 2] = (hidden[...] * pair_all[HALF : HALF + 1].astype(F32)).astype(BF16)

    def small(kind, src, dst, k, peer):
        copy = remote(src, dst, small_send.at[kind, k], small_recv.at[kind, k], peer)
        copy.start()
        return copy

    def gather(orders):
        rings, shared = [], []

        def share(part, index, at):
            ref = view(rows_buf, at, ALL, LANES[part], (side,))
            copy = remote(ref, ref, share_send.at[part, index], share_recv.at[part, index], sibling)
            copy.start()
            shared.append(copy)

        square_copies, inverse_copies = [], []
        for phase in range(3):
            now = []
            for part in range(3):
                axis = orders[part][phase]
                own = {a: here[a] for a in orders[part][phase:]}
                bundle = lambda j, rows, part=part, own=own, axis=axis: view(
                    rows_buf, {**own, axis: j}, rows, LANES[part], (side,)
                )
                ring = RingGather(
                    here, axis, bundle, (send_sems.at[0, part, phase], recv_sems.at[0, part, phase])
                )
                ring.start()
                if phase == 2:
                    share(part, 0, own)
                now.append((part, axis, own, ring))
            if phase == 0:
                value = hidden[...]
                columns[0:HALF] = jnp.broadcast_to(
                    jnp.sum(value * value, axis=1, keepdims=True), (HALF, 128)
                )
                columns[HALF:128] = jnp.zeros((HALF, 128), F32)
                squares[row] = columns[...].T[0:8]
                for k in range(7):
                    square_copies.append(small(1, squares.at[row], squares.at[row], k, row_peers[k]))
            if phase == 1:
                for copy in square_copies:
                    copy.wait_recv()
                sums = squares[0]
                for k in range(1, 8):
                    sums = sums + squares[k]
                inverses[side, col] = lax.rsqrt(sums / D + 1e-06)
                for k in range(7):
                    place = inverses.at[side, col]
                    inverse_copies.append(small(2, place, place, k, col_peers[k]))
            if phase == 2:
                for copy in inverse_copies:
                    copy.wait_recv()
                place = inverses.at[side]
                inverse_share = remote(place, place, pair_sems.at[4], pair_sems.at[5], sibling)
                inverse_share.start()
            for part, axis, own, ring in now:
                ring.relay()
            if phase == 2:
                load_down.wait()
                for r in range(8):
                    for core in range(2):
                        down_pairs[r, :, core * OWN : (core + 1) * OWN] = down[
                            :, (core * 8 + r) * OWN : (core * 8 + r + 1) * OWN
                        ]
            for part, axis, own, ring in now:
                ring.near()
                if phase == 2:
                    share(part, 1, {**own, axis: (here[axis] + 3) % 4})
                    share(part, 2, {**own, axis: (here[axis] + 1) % 4})
            for part, axis, own, ring in now:
                ring.far()
                if phase == 2:
                    share(part, 3, {**own, axis: (here[axis] + 2) % 4})
                rings.append(ring)
        for copy in shared:
            copy.wait_recv()
        inverse_share.wait()
        for ring in rings:
            ring.drain()
        for copy in shared + square_copies + inverse_copies:
            copy.wait_send()

    for core in range(2):
        @pl.when(side == core)
        def _(core=core):
            gather(ORDERS[core])

    for copy in gate_copies:
        copy.wait()
    columns[...] = jnp.zeros_like(columns)
    for c in range(8):
        columns[c : c + 1] = gates[c, 0:1]
        columns[8 + c : 9 + c] = inverses[side, c, 0:1]
        columns[16 + c : 17 + c] = inverses[1 - side, c, 0:1]
    columns[...] = columns[...].T
    for load in loads:
        load.wait()

    def experts(half, place):
        total[...] = jnp.zeros_like(total)

        @pl.loop(0, 8)
        def _(r):
            lhs = rows_buf[half, :, :, :, r // 4, r // 2 % 2, r % 2].reshape(8 * HALF, PAIR)
            total[...] += jnp.dot(lhs, weights[r].reshape(PAIR, 512), preferred_element_type=F32)

        gate_rows = columns[pl.ds(pl.multiple_of(half * HALF, HALF), HALF), 0:8]
        scales = columns[0:HALF]
        acts = []
        for c in range(8):
            scale = scales[:, place + c : place + c + 1]
            gate_part = total[c * HALF : (c + 1) * HALF, :256] * scale
            up_part = total[c * HALF : (c + 1) * HALF, 256:] * (scale * gate_rows[:, c : c + 1])
            acts.append((gate_part / (1.0 + jnp.exp(-gate_part)) * up_part).astype(BF16))
        return jnp.concatenate(acts, axis=0)

    theirs_act = experts(1 - side, 16)

    def back(r):
        return remote(
            rows_buf.at[1 - side, :, :, :, r // 4, r // 2 % 2, r % 2],
            from_sibling.at[r],
            back_send.at[r],
            back_recv.at[r],
            sibling,
        )

    @pl.loop(0, 8)
    def _(r):
        value = jnp.dot(theirs_act, down_pairs[r], preferred_element_type=F32).astype(BF16)
        rows_buf[1 - side, :, :, :, r // 4, r // 2 % 2, r % 2] = value.reshape(2, 2, 2, HALF, PAIR)
        back(r).start()

    own_act = experts(side, 8)

    @pl.loop(0, 8)
    def _(r):
        value = jnp.dot(own_act, down_pairs[r], preferred_element_type=F32)
        back(r).wait_recv()
        value = value + from_sibling[r].reshape(8 * HALF, PAIR).astype(F32)
        rows_buf[side, :, :, :, r // 4, r // 2 % 2, r % 2] = value.astype(BF16).reshape(2, 2, 2, HALF, PAIR)

    def scatter(orders):
        rings = []
        for phase in range(3):
            now = []
            for part in range(3):
                axis = orders[part][phase]
                done = {a: here[a] for a in orders[part][:phase]}
                bundle = lambda j, rows, part=part, done=done, axis=axis: view(
                    rows_buf, {**done, axis: j}, rows, LANES[part], (side,)
                )
                ring = RingScatter(
                    here,
                    axis,
                    bundle,
                    arrivals[part * 3 + phase],
                    (send_sems.at[1, part, phase], recv_sems.at[1, part, phase]),
                )
                ring.start()
                now.append((part, ring))
            for part, ring in now:
                ring.relay()
            for part, ring in now:
                if phase < 2:
                    ring.finish()
                else:

                    def use(rows, value, part=part):
                        spot = (pl.ds(*rows), pl.ds(*LANES[part]))
                        mixed[spot] = (hidden[spot] + value).astype(BF16)

                    ring.finish(use)
                rings.append(ring)
        for ring in rings:
            ring.drain()

    for core in range(2):
        @pl.when(side == core)
        def _(core=core):
            scatter(ORDERS[core])

    last = remote(mixed, mixed_sib, pair_sems.at[6], pair_sems.at[7], sibling)
    last.start()
    last.wait_recv()

    @pl.when(side == 0)
    def _():
        out_ref[0:HALF] = mixed[:, 0:OWN]
        out_ref[HALF : 2 * HALF] = mixed_sib[:, 0:OWN]

    @pl.when(side == 1)
    def _():
        out_ref[0:HALF] = mixed_sib[:, OWN:PAIR]
        out_ref[HALF : 2 * HALF] = mixed[:, OWN:PAIR]

    last.wait_send()
    for ring in (ring_first, ring_second, early_ring, late_ring):
        ring.drain()
    for copy in (flip_first, flip_second, early_flip, late_flip, pair_copy, proj_copy, head_share):
        copy.wait_send()

    @pl.loop(0, 8)
    def _(r):
        back(r).wait_send()


ARRIVALS = [
    (2, 3, *(2,) * (4 - 2 * phase), 32, LANES[part][1]) for part in range(3) for phase in range(3)
]

VMEM = pl.BlockSpec(memory_space=pltpu.VMEM)
ANY = pl.BlockSpec(memory_space=pl.ANY)
DMA = pltpu.SemaphoreType.DMA


def layer_call(head_out, pair, gate_tile, w_out, w_gate, w_up, w_down):
    scratch = [
        pltpu.VMEM((2, 2, 2, 2, HALF, 2048), BF16),
        pltpu.VMEM((2, 2048, OWN), BF16),
        pltpu.VMEM((2, 4, HALF, PAIR), BF16),
        pltpu.VMEM((4, HALF, SUM_LANES[1][1]), BF16),
        pltpu.VMEM((HALF, SUM_LANES[0][1]), BF16),
        pltpu.VMEM((2, 3, 2, 32, SUM_LANES[0][1]), BF16),
        pltpu.VMEM((2, 3, 32, SUM_LANES[1][1]), BF16),
        pltpu.VMEM((80, OWN), BF16),
        pltpu.VMEM((80, PAIR), BF16),
        pltpu.VMEM((HALF, PAIR), F32),
        pltpu.VMEM((2, 2, 2, 2, 2, 2, 2, HALF, PAIR), BF16),
        pltpu.VMEM((8, 2, OWN, 512), BF16),
        pltpu.VMEM((256, D), BF16),
        pltpu.VMEM((8, 256, PAIR), BF16),
        pltpu.VMEM((8 * HALF, 512), F32),
        pltpu.VMEM((8, 8, 128), F32),
        pltpu.VMEM((2, 8, 8, 128), F32),
        pltpu.VMEM((8, 8, 128), F32),
        pltpu.VMEM((128, 128), F32),
        pltpu.VMEM((8, 2, 2, 2, HALF, PAIR), BF16),
        pltpu.VMEM((HALF, PAIR), BF16),
        pltpu.VMEM((HALF, PAIR), BF16),
        DMA((6,)),
        DMA((2, 2, 2, 3)),
        DMA((2, 4)),
        DMA((2, 2, 2, 3)),
        DMA((8,)),
        DMA((2,)),
        DMA((3, 7)),
        DMA((3, 7)),
        DMA((2, 3, 3, 2, 3)),
        DMA((2, 3, 3, 2, 3)),
        DMA((3, 4)),
        DMA((3, 4)),
        DMA((8,)),
        DMA((8,)),
        *[pltpu.VMEM(shape, BF16) for shape in ARRIVALS],
    ]
    return pl.pallas_call(
        layer_kernel,
        out_shape=jax.ShapeDtypeStruct((2 * HALF, OWN), BF16),
        in_specs=[VMEM, VMEM, VMEM, ANY, ANY, ANY, ANY],
        out_specs=VMEM,
        scratch_shapes=scratch,
        compiler_params=pltpu.CompilerParams(
            collective_id=0, has_side_effects=True, vmem_limit_bytes=58 * 2**20
        ),
        cost_estimate=pl.CostEstimate(
            flops=2 * 1024 * 7168 * 1000, bytes_accessed=16 * 2**20, transcendentals=2**18
        ),
    )(head_out, pair, gate_tile, w_out, w_gate, w_up, w_down)


def shards(
    queries,
    cache,
    lengths,
    w_uv,
    w_out,
    residual_in,
    norm_gain,
    expert_ids,
    gate_vals,
    w_gate,
    w_up,
    w_down,
):
    owner_index = lax.axis_index(("side", "row"))
    my_gate = jnp.sum(jnp.where(expert_ids == owner_index, gate_vals, 0.0), axis=1)
    gate_tile = jnp.broadcast_to(my_gate[None, :], (8, 128))
    pair = jnp.concatenate(
        [residual_in.reshape(2, HALF, OWN), jnp.broadcast_to(norm_gain, (2, 16, OWN))], axis=1
    )

    score_scale = (HD + ROPE) ** (-0.5)
    scores = (
        jnp.einsum("rhk,rlk->rhl", queries, cache, preferred_element_type=jnp.float32) * score_scale
    )
    places = lax.broadcasted_iota(jnp.int32, (1, 1, cache.shape[1]), 2)
    scores = jnp.where(places < lengths[:, None, None], scores, -jnp.inf)
    row_top = jnp.max(scores, axis=2, keepdims=True)
    exp_terms = jnp.exp(scores - row_top)
    attn_probs = (exp_terms / jnp.sum(exp_terms, axis=2, keepdims=True)).astype(jnp.bfloat16)
    latent_width = w_uv.shape[1]
    latent = jnp.einsum(
        "rhl,rlk->rhk", attn_probs, cache[:, :, :latent_width], preferred_element_type=jnp.float32
    ).astype(jnp.bfloat16)
    head_out = jnp.einsum("rhk,hkd->rhd", latent, w_uv, preferred_element_type=jnp.float32).astype(
        jnp.bfloat16
    )
    head_out = head_out.reshape(head_out.shape[0], -1)
    return layer_call(
        head_out,
        pair,
        gate_tile,
        w_out,
        w_gate.reshape(2, 8, OWN, 256),
        w_up.reshape(2, 8, OWN, 256),
        w_down[0],
    )


def solution(mesh):
    placed = (
        P(("side", "row"), "col", None),
        P(("side", "row"), None, None),
        P(("side", "row")),
        P("col", None, None),
        P("col", ("side", "row")),
        P("col", ("side", "row")),
        P(("side", "row")),
        P("col", None),
        P("col", None),
        P(("side", "row"), None, "col"),
        P(("side", "row"), None, "col"),
        P(("side", "row"), "col", None),
    )
    return jax.shard_map(
        shards, mesh=mesh, in_specs=placed, out_specs=P("col", ("side", "row")), check_vma=False
    )
```

```python
import jax
import jax.numpy as jnp
from jax import lax
from jax.experimental import pallas as pl
from jax.experimental.pallas import tpu as pltpu
from jax.sharding import PartitionSpec as P

D = 7168
ROPE = 64
HD = 128
HALF = 64
OWN = 448
PAIR = 896
MESH = pl.DeviceIdType.MESH
BF16 = jnp.bfloat16
F32 = jnp.float32

LANES = ((0, 384), (384, 256), (640, 256))
ORDERS = (
    (("x", "y", "z"), ("y", "z", "x"), ("z", "x", "y")),
    (("y", "z", "x"), ("z", "x", "y"), ("x", "y", "z")),
)
HEAD_LANES = ((0, 1152), (1152, 896))
SUM_LANES = ((0, 512), (512, 384))
LOW, HIGH, ALL = (0, 32), (32, 32), (0, 64)


class Place:
    def __init__(self):
        self.side, self.row, self.col = (lax.axis_index(name) for name in ("side", "row", "col"))
        z_hi, y = lax.div(self.row, 4), lax.rem(self.row, 4)
        z_lo, x = lax.div(self.col, 4), lax.rem(self.col, 4)
        at = {"x": x, "y": y, "z": z_hi * 2 + z_lo}
        self.coord = {a: [at[a]] + [lax.rem(at[a] + k, 4) for k in (1, 2, 3)] for a in "xyz"}
        self.bits = {a: [(lax.div(j, 2), lax.rem(j, 2)) for j in self.coord[a]] for a in "xyz"}
        self.sibling = (1 - self.side, self.row, self.col)
        self.ids = {"x": [], "y": [], "z": []}
        for k in range(4):
            high, low = self.bits["z"][k]
            self.ids["x"].append((self.side, self.row, z_lo * 4 + self.coord["x"][k]))
            self.ids["y"].append((self.side, z_hi * 4 + self.coord["y"][k], self.col))
            self.ids["z"].append((self.side, high * 4 + y, low * 4 + x))

    def view(self, ref, at, rows, lanes, lead=()):
        index = [slice(None)] * 6
        if "x" in at:
            index[1], index[2] = self.bits["x"][at["x"]]
        if "y" in at:
            index[4], index[5] = self.bits["y"][at["y"]]
        if "z" in at:
            index[3], index[0] = self.bits["z"][at["z"]]
        return ref.at[(*lead, *index, pl.ds(*rows), pl.ds(*lanes))]


def remote(src, dst, send_sem, recv_sem, device):
    return pltpu.make_async_remote_copy(
        src_ref=src,
        dst_ref=dst,
        send_sem=send_sem,
        recv_sem=recv_sem,
        device_id=device,
        device_id_type=MESH,
    )


class RingGather:
    def __init__(self, here, axis, bundle, halves, sems):
        self.here, self.axis, self.bundle, self.halves, self.sems = here, axis, bundle, halves, sems

    def copy(self, direction, piece):
        send, recv = self.sems
        up = (1, 3)[direction]
        half = self.halves[direction if piece != 1 else 1 - direction]
        ref = self.bundle(0 if piece < 2 else 4 - up, half)
        device = self.here.ids[self.axis][up]
        return remote(ref, ref, send.at[direction, piece], recv.at[direction, piece], device)

    def start(self):
        for piece in range(2):
            for direction in range(2):
                self.copy(direction, piece).start()

    def relay(self):
        for direction in range(2):
            self.copy(direction, 0).wait_recv()
            self.copy(direction, 2).start()

    def near(self):
        for direction in range(2):
            self.copy(direction, 1).wait_recv()

    def far(self):
        for direction in range(2):
            self.copy(direction, 2).wait_recv()

    def drain(self):
        for direction in range(2):
            for piece in range(3):
                self.copy(direction, piece).wait_send()


class RingScatter:
    def __init__(self, here, axis, bundle, halves, arrived, sems):
        self.here, self.axis, self.bundle, self.halves = here, axis, bundle, halves
        self.arrived, self.sems = arrived, sems

    def place(self, direction, piece):
        k = 2 if piece == 0 else (1, 3)[direction]
        return self.bundle(k, self.halves[direction if piece != 1 else 1 - direction])

    def copy(self, direction, piece):
        send, recv = self.sems
        return remote(
            self.place(direction, piece),
            self.arrived.at[direction, piece],
            send.at[direction, piece],
            recv.at[direction, piece],
            self.here.ids[self.axis][(1, 3)[direction]],
        )

    def start(self):
        for piece in range(2):
            for direction in range(2):
                self.copy(direction, piece).start()

    def relay(self):
        for direction in range(2):
            self.copy(direction, 0).wait_recv()
            target = self.place(direction, 2)
            target[...] = (target[...].astype(F32) + self.arrived[direction, 0].astype(F32)).astype(BF16)
            self.copy(direction, 2).start()

    def finish(self, use=None):
        for direction in range(2):
            self.copy(direction, 1).wait_recv()
            self.copy(direction, 2).wait_recv()
        for rows, (first, second) in zip(self.halves, ((2, 1), (1, 2))):
            target = self.bundle(0, rows)
            value = target[...].astype(F32) + (
                self.arrived[0, first].astype(F32) + self.arrived[1, second].astype(F32)
            )
            if use is None:
                target[...] = value.astype(BF16)
            else:
                use(rows, value)

    def drain(self):
        for direction in range(2):
            for piece in range(3):
                self.copy(direction, piece).wait_send()


def layer_kernel(
    head_ref, residual_ref, gain_ref, ids_ref, vals_ref, out_hbm, gate_hbm, up_hbm, down_hbm, out_ref,
    heads, proj, part_sums, z_early, z_late, x_early, x_late, pair, pair_sib, pair_all, hidden, square,
    rows_buf, weights, down, down_pairs, total, acts, squares, inverses, gates, columns,
    from_sibling, mixed, mixed_sib,
    load_sems, head_sems, flip_sems, sum_sems, pair_sems, proj_sems, small_send, small_recv,
    send_sems, recv_sems, share_send, share_recv, back_send, back_recv, *arrivals,
):
    here = Place()
    side, row, col, sibling = here.side, here.row, here.col, here.sibling
    (z_hi, z_lo), (x_hi, x_lo), (y_hi, y_lo) = (here.bits[axis][0] for axis in "zxy")
    x = here.coord["x"][0]
    far_z = here.ids["z"][2]
    flip_z = (side, row, lax.rem(col + 4, 8))

    def row_peer(k):
        return (side, lax.rem(row + k, 8), col)

    def col_peer(k):
        return (side, row, lax.rem(col + k, 8))


    loads = [
        pltpu.make_async_copy(
            source.at[core],
            weights.at[:, core, :, pl.ds(which * 256, 256)],
            load_sems.at[which * 2 + core],
        )
        for which, source in enumerate((gate_hbm, up_hbm))
        for core in range(2)
    ]
    load_proj = pltpu.make_async_copy(out_hbm, proj.at[side], load_sems.at[4])
    load_down = pltpu.make_async_copy(down_hbm, down, load_sems.at[5])
    heads[side, z_hi, y_hi, y_lo] = head_ref[...]

    barrier = pltpu.get_barrier_semaphore()
    peers = [sibling, *map(row_peer, range(1, 8)), *map(col_peer, range(1, 8)), here.ids["z"][1], here.ids["z"][3]]
    for peer in peers:
        pl.semaphore_signal(barrier, inc=1, device_id=peer, device_id_type=MESH)
    pl.semaphore_wait(barrier, len(peers))

    def head_view(which, at, rows):
        return heads.at[(side, *at, pl.ds(*rows), pl.ds(*HEAD_LANES[which]))]

    def head_ring(index, which, z):
        return RingGather(
            here,
            "y",
            lambda k, rows: head_view(which, (z, *here.bits["y"][k]), rows),
            (LOW, HIGH),
            (head_sems.at[0, index], head_sems.at[1, index]),
        )

    def head_flip(index, which, k):
        ref = head_view(which, (z_hi, *here.bits["y"][k]), ALL)
        return remote(ref, ref, flip_sems.at[0, index], flip_sems.at[1, index], far_z)

    flips = [head_flip(0, 0, 0)] + [head_flip(1 + k, 1, k) for k in range(4)]
    rings = [head_ring(0, 1, z_hi), head_ring(1, 0, z_hi), head_ring(2, 0, 1 - z_hi)]
    flips[0].start()
    rings[0].start()
    rings[1].start()
    flips[1].start()
    load_proj.start()
    for load in loads:
        load.start()
    load_down.start()

    owner = side * 8 + row
    chosen = jnp.where(ids_ref[...] == owner, vals_ref[...], 0.0)
    gates[col] = jnp.broadcast_to(jnp.sum(chosen, axis=0, keepdims=True), (8, 128))
    square[0:OWN] = residual_ref[...].astype(F32)
    square[OWN:512] = jnp.zeros((512 - OWN, 128), F32)
    residual = square[...].T.astype(BF16)
    for half in range(2):
        pair[half, 0:HALF] = residual[half * HALF : (half + 1) * HALF, 0:OWN]
        pair[half, HALF:80] = jnp.broadcast_to(gain_ref[...].astype(F32), (16, OWN)).astype(BF16)
    pair_copy = remote(pair.at[1 - side], pair_sib, pair_sems.at[0], pair_sems.at[1], sibling)
    pair_copy.start()
    proj_copy = remote(out_hbm, proj.at[side], proj_sems.at[0], proj_sems.at[1], sibling)
    proj_copy.start()
    def smalls(kind, ref, name):
        @pl.loop(0, 7)
        def _(k):
            peer = row_peer(k + 1) if kind == 1 else col_peer(k + 1)
            getattr(remote(ref, ref, small_send.at[kind, k], small_recv.at[kind, k], peer), name)()

    smalls(0, gates.at[col], "start")

    rings[0].relay()
    flips[0].wait_recv()
    rings[2].start()
    rings[0].near()
    flips[2].start()
    flips[4].start()
    rings[1].relay()
    rings[0].far()
    flips[3].start()

    pair_copy.wait_recv()

    @pl.when(side == 0)
    def _():
        pair_all[:, 0:OWN] = pair[0]
        pair_all[:, OWN:PAIR] = pair_sib[...]

    @pl.when(side == 1)
    def _():
        pair_all[:, 0:OWN] = pair_sib[...]
        pair_all[:, OWN:PAIR] = pair[1]

    rings[2].relay()
    for ring in rings[1:]:
        ring.near()
        ring.far()
    for flip in flips[1:]:
        flip.wait_recv()
    theirs = heads.at[side, :, :, 1 - side]
    head_share = remote(theirs, theirs, pair_sems.at[2], pair_sems.at[3], sibling)
    head_share.start()

    load_proj.wait()
    proj_copy.wait_recv()

    def project(source):
        lhs = heads[source, :, :, side].reshape(4 * HALF, 2048)
        value = lax.dot_general(
            lhs, proj[...].reshape(PAIR, 2048), (((1,), (1,)), ((), ())), preferred_element_type=F32
        )
        part_sums[source] = value.astype(BF16).reshape(4, HALF, PAIR)

    project(side)
    head_share.wait_recv()
    project(1 - side)

    def x_ring(which, lead, arrived):
        return RingScatter(
            here,
            "x",
            lambda k, rows: part_sums.at[lead, here.coord["x"][k], pl.ds(*rows), pl.ds(*SUM_LANES[which])],
            (LOW, HIGH),
            arrived,
            (sum_sems.at[0, which], sum_sems.at[1, which]),
        )

    early_flip = remote(
        part_sums.at[1 - z_lo, :, :, pl.ds(*SUM_LANES[1])], z_early, flip_sems.at[0, 5], flip_sems.at[1, 5], flip_z
    )
    early_flip.start()
    early_ring = x_ring(0, slice(None), x_early)
    early_ring.start()
    early_ring.relay()
    early_flip.wait_recv()
    mine = part_sums.at[z_lo, :, :, pl.ds(*SUM_LANES[1])]
    mine[...] = (mine[...].astype(F32) + z_early[...].astype(F32)).astype(BF16)
    late_ring = x_ring(1, z_lo, x_late)
    late_ring.start()
    early_ring.finish()
    late_flip = remote(
        part_sums.at[1 - z_lo, x, :, pl.ds(*SUM_LANES[0])], z_late, flip_sems.at[0, 6], flip_sems.at[1, 6], flip_z
    )
    late_flip.start()
    late_ring.relay()
    late_flip.wait_recv()
    left = pl.ds(*SUM_LANES[0])
    hidden[:, left] = pair_all[0:HALF, left].astype(F32) + (
        part_sums[z_lo, x, :, left].astype(F32) + z_late[...].astype(F32)
    )

    def right(rows, value):
        spot = (pl.ds(*rows), pl.ds(*SUM_LANES[1]))
        hidden[spot] = pair_all[spot].astype(F32) + value

    late_ring.finish(right)
    rows_buf[side, z_lo, x_hi, x_lo, z_hi, y_hi, y_lo] = (
        hidden[...] * pair_all[HALF : HALF + 1].astype(F32)
    ).astype(BF16)

    def per_core(step):
        for core in range(2):

            @pl.when(side == core)
            def _(core=core):
                step(ORDERS[core])

    def halves(t):
        return (t * 32, 16), (t * 32 + 16, 16)

    def gather_rings(t, phase, orders):
        for part in range(3):
            axis = orders[part][phase]
            own = {a: 0 for a in orders[part][phase:]}
            yield RingGather(
                here,
                axis,
                lambda k, rows, part=part, own=own, axis=axis: here.view(
                    rows_buf, {**own, axis: k}, rows, LANES[part], (side,)
                ),
                halves(t),
                (send_sems.at[0, t, part, phase], recv_sems.at[0, t, part, phase]),
            )

    def scatter_rings(t, phase, orders):
        for part in range(3):
            axis = orders[part][phase]
            done = {a: 0 for a in orders[part][:phase]}
            yield RingScatter(
                here,
                axis,
                lambda k, rows, part=part, done=done, axis=axis: here.view(
                    rows_buf, {**done, axis: k}, rows, LANES[part], (side,)
                ),
                halves(t),
                arrivals[part * 3 + phase].at[t],
                (send_sems.at[1, t, part, phase], recv_sems.at[1, t, part, phase]),
            )

    def each(rings, *names):
        def step(orders):
            made = list(rings(orders))
            for name in names:
                for ring in made:
                    getattr(ring, name)()

        per_core(step)

    def gather(t, phase, *names):
        each(lambda orders: gather_rings(t, phase, orders), *names)

    def scatter(t, phase, *names):
        each(lambda orders: scatter_rings(t, phase, orders), *names)

    def share(t, part, k, orders):
        ref = here.view(rows_buf, {orders[part][2]: k}, (t * 32, 32), LANES[part], (side,))
        return remote(ref, ref, share_send.at[t, part, k], share_recv.at[t, part, k], sibling)

    def shares(t, steps, name):
        def step(orders):
            for part in range(3):
                for k in steps:
                    getattr(share(t, part, k, orders), name)()

        per_core(step)

    def chunk(r):
        return lax.div(r, 4), lax.rem(lax.div(r, 2), 2), lax.rem(r, 2)

    def back(t, r):
        return remote(
            rows_buf.at[(1 - side,) + (slice(None),) * 3 + chunk(r) + (pl.ds(t * 32, 32),)],
            from_sibling.at[t, r],
            back_send.at[t, r],
            back_recv.at[t, r],
            sibling,
        )

    def experts(t):
        total[...] = jnp.zeros_like(total)

        @pl.loop(0, 8)
        def _(r):
            lhs = rows_buf[(slice(None),) * 4 + chunk(r) + (pl.ds(t * 32, 32),)].reshape(512, PAIR)
            total[...] += jnp.dot(lhs, weights[r].reshape(PAIR, 512), preferred_element_type=F32)

        for half in range(2):
            for c in range(8):
                first = half * 256 + c * 32
                scale = columns[t * 32 : t * 32 + 32, 8 + half * 8 + c : 9 + half * 8 + c]
                gate_col = columns[half * HALF + t * 32 : half * HALF + t * 32 + 32, c : c + 1]
                gate_part = total[first : first + 32, :256] * scale
                up_part = total[first : first + 32, 256:] * (scale * gate_col)
                acts[half, c * 32 : c * 32 + 32] = (
                    gate_part / (1.0 + jnp.exp(-gate_part)) * up_part
                ).astype(BF16)

    def down_theirs(t):
        @pl.loop(0, 8)
        def _(r):
            value = jnp.dot(acts[1 - side], down_pairs[r], preferred_element_type=F32).astype(BF16)
            rows_buf[(1 - side,) + (slice(None),) * 3 + chunk(r) + (pl.ds(t * 32, 32),)] = value.reshape(2, 2, 2, 32, PAIR)
            back(t, r).start()

    def down_own(t):
        @pl.loop(0, 8)
        def _(r):
            value = jnp.dot(acts[side], down_pairs[r], preferred_element_type=F32)
            back(t, r).wait_recv()
            value = value + from_sibling[t, r].reshape(256, PAIR).astype(F32)
            rows_buf[(side,) + (slice(None),) * 3 + chunk(r) + (pl.ds(t * 32, 32),)] = value.astype(BF16).reshape(
                2, 2, 2, 32, PAIR
            )

    def final(t):
        def step(orders):
            for part, ring in enumerate(scatter_rings(t, 2, orders)):

                def use(rows, value, part=part):
                    spot = (pl.ds(*rows), pl.ds(*LANES[part]))
                    mixed[spot] = (hidden[spot] + value).astype(BF16)

                ring.finish(use)

        per_core(step)

    gather(0, 0, "start")
    gather(1, 0, "start")
    value = hidden[...]
    columns[0:HALF] = jnp.broadcast_to(jnp.sum(value * value, axis=1, keepdims=True), (HALF, 128))
    columns[HALF:128] = jnp.zeros((HALF, 128), F32)
    squares[row] = columns[...].T[0:8]
    smalls(1, squares.at[row], "start")
    gather(0, 0, "relay")
    gather(1, 0, "relay")
    gather(0, 0, "near", "far")
    gather(0, 1, "start")
    gather(1, 0, "near", "far")
    gather(1, 1, "start")
    smalls(1, squares.at[row], "wait_recv")
    inverses[side, col] = lax.rsqrt(jnp.sum(squares[...], axis=0) / D + 1e-06)
    smalls(2, inverses.at[side, col], "start")
    gather(0, 1, "relay")
    gather(0, 1, "near")
    gather(1, 1, "relay")
    gather(0, 1, "far")
    gather(0, 2, "start")
    shares(0, (0,), "start")
    gather(1, 1, "near", "far")
    smalls(2, inverses.at[side, col], "wait_recv")
    inverse_share = remote(
        inverses.at[side], inverses.at[side], pair_sems.at[4], pair_sems.at[5], sibling
    )
    inverse_share.start()
    load_down.wait()
    for r in range(8):
        for core in range(2):
            down_pairs[r, :, core * OWN : (core + 1) * OWN] = down[
                :, (core * 8 + r) * OWN : (core * 8 + r + 1) * OWN
            ]
    gather(0, 2, "relay")
    gather(1, 2, "start")
    shares(1, (0,), "start")
    gather(0, 2, "near")
    shares(0, (1, 3), "start")
    smalls(0, gates.at[col], "wait_recv")
    inverse_share.wait_recv()
    columns[...] = jnp.zeros_like(columns)
    for c in range(8):
        columns[c : c + 1] = gates[c, 0:1]
        columns[8 + c : 9 + c] = inverses[0, c, 0:1]
        columns[16 + c : 17 + c] = inverses[1, c, 0:1]
    columns[...] = columns[...].T
    for load in loads:
        load.wait()
    gather(0, 2, "far")
    shares(0, (2,), "start")
    shares(0, (0, 1, 2, 3), "wait_recv")
    experts(0)
    gather(1, 2, "relay")
    down_theirs(0)
    gather(1, 2, "near")
    shares(1, (1, 3), "start")
    for phase in range(3):
        gather(0, phase, "drain")
    shares(0, (0, 1, 2, 3), "wait_send")
    down_own(0)
    gather(1, 2, "far")
    shares(1, (2,), "start")
    scatter(0, 0, "start")
    shares(1, (0, 1, 2, 3), "wait_recv")
    experts(1)
    scatter(0, 0, "relay")
    down_theirs(1)
    for phase in range(3):
        gather(1, phase, "drain")
    shares(1, (0, 1, 2, 3), "wait_send")
    down_own(1)
    scatter(1, 0, "start")
    scatter(0, 0, "finish")
    scatter(0, 1, "start")
    scatter(1, 0, "relay")
    scatter(0, 1, "relay")
    scatter(0, 1, "finish")
    scatter(0, 2, "start")
    scatter(0, 2, "relay")
    scatter(1, 0, "finish")
    scatter(1, 1, "start")
    final(0)
    scatter(1, 1, "relay", "finish")
    scatter(1, 2, "start", "relay")
    final(1)

    last = remote(mixed, mixed_sib, pair_sems.at[6], pair_sems.at[7], sibling)
    last.start()
    last.wait_recv()

    def transposed(top, bottom):
        square[0:PAIR // 2, 0:HALF] = top.astype(F32).T
        square[0:PAIR // 2, HALF:128] = bottom.astype(F32).T
        out_ref[...] = square[0:OWN].astype(BF16)

    @pl.when(side == 0)
    def _():
        transposed(mixed[:, 0:OWN], mixed_sib[:, 0:OWN])

    @pl.when(side == 1)
    def _():
        transposed(mixed_sib[:, OWN:PAIR], mixed[:, OWN:PAIR])

    last.wait_send()
    for ring in (*rings, early_ring, late_ring):
        ring.drain()
    for copy in (
        *flips, early_flip, late_flip, pair_copy, proj_copy, head_share, inverse_share,
    ):
        copy.wait_send()
    smalls(0, gates.at[col], "wait_send")
    smalls(1, squares.at[row], "wait_send")
    smalls(2, inverses.at[side, col], "wait_send")
    for t in range(2):
        for phase in range(3):
            scatter(t, phase, "drain")

        @pl.loop(0, 8)
        def _(r, t=t):
            back(t, r).wait_send()


ARRIVALS = [
    (2, 2, 3, *(2,) * (4 - 2 * phase), 16, LANES[part][1]) for part in range(3) for phase in range(3)
]

VMEM = pl.BlockSpec(memory_space=pltpu.VMEM)
ANY = pl.BlockSpec(memory_space=pl.ANY)
DMA = pltpu.SemaphoreType.DMA


def layer_call(*args):
    scratch = [
        pltpu.VMEM((2, 2, 2, 2, HALF, 2048), BF16),
        pltpu.VMEM((2, OWN, 2048), BF16),
        pltpu.VMEM((2, 4, HALF, PAIR), BF16),
        pltpu.VMEM((4, HALF, SUM_LANES[1][1]), BF16),
        pltpu.VMEM((HALF, SUM_LANES[0][1]), BF16),
        pltpu.VMEM((2, 3, 2, 32, SUM_LANES[0][1]), BF16),
        pltpu.VMEM((2, 3, 32, SUM_LANES[1][1]), BF16),
        pltpu.VMEM((2, 80, OWN), BF16),
        pltpu.VMEM((80, OWN), BF16),
        pltpu.VMEM((80, PAIR), BF16),
        pltpu.VMEM((HALF, PAIR), F32),
        pltpu.VMEM((512, 128), F32),
        pltpu.VMEM((2, 2, 2, 2, 2, 2, 2, HALF, PAIR), BF16),
        pltpu.VMEM((8, 2, OWN, 512), BF16),
        pltpu.VMEM((256, D), BF16),
        pltpu.VMEM((8, 256, PAIR), BF16),
        pltpu.VMEM((512, 512), F32),
        pltpu.VMEM((2, 256, 256), BF16),
        pltpu.VMEM((8, 8, 128), F32),
        pltpu.VMEM((2, 8, 8, 128), F32),
        pltpu.VMEM((8, 8, 128), F32),
        pltpu.VMEM((128, 128), F32),
        pltpu.VMEM((2, 8, 2, 2, 2, 32, PAIR), BF16),
        pltpu.VMEM((HALF, PAIR), BF16),
        pltpu.VMEM((HALF, PAIR), BF16),
        DMA((6,)),
        DMA((2, 3, 2, 3)),
        DMA((2, 7)),
        DMA((2, 2, 2, 3)),
        DMA((8,)),
        DMA((2,)),
        DMA((3, 7)),
        DMA((3, 7)),
        DMA((2, 2, 3, 3, 2, 3)),
        DMA((2, 2, 3, 3, 2, 3)),
        DMA((2, 3, 4)),
        DMA((2, 3, 4)),
        DMA((2, 8)),
        DMA((2, 8)),
        *[pltpu.VMEM(shape, BF16) for shape in ARRIVALS],
    ]
    return pl.pallas_call(
        layer_kernel,
        out_shape=jax.ShapeDtypeStruct((OWN, 2 * HALF), BF16),
        in_specs=[VMEM] * 5 + [ANY] * 4,
        out_specs=VMEM,
        scratch_shapes=scratch,
        compiler_params=pltpu.CompilerParams(
            collective_id=0, has_side_effects=True, vmem_limit_bytes=58 * 2**20
        ),
        cost_estimate=pl.CostEstimate(
            flops=2 * 1024 * 7168 * 1000, bytes_accessed=16 * 2**20, transcendentals=2**18
        ),
    )(*args)


def shards(
    queries,
    cache,
    lengths,
    w_uv,
    w_out,
    residual_in,
    norm_gain,
    expert_ids,
    gate_vals,
    w_gate,
    w_up,
    w_down,
):
    score_scale = (HD + ROPE) ** (-0.5)
    scores = (
        jnp.einsum("rhk,rlk->rhl", queries, cache, preferred_element_type=jnp.float32) * score_scale
    )
    places = lax.broadcasted_iota(jnp.int32, (1, 1, cache.shape[1]), 2)
    scores = jnp.where(places < lengths[:, None, None], scores, -jnp.inf)
    row_top = jnp.max(scores, axis=2, keepdims=True)
    exp_terms = jnp.exp(scores - row_top)
    attn_probs = (exp_terms / jnp.sum(exp_terms, axis=2, keepdims=True)).astype(jnp.bfloat16)
    latent_width = w_uv.shape[1]
    latent = jnp.einsum(
        "rhl,rlk->rhk", attn_probs, cache[:, :, :latent_width], preferred_element_type=jnp.float32
    ).astype(jnp.bfloat16)
    head_out = jnp.einsum("rhk,hkd->rhd", latent, w_uv, preferred_element_type=jnp.float32).astype(
        jnp.bfloat16
    )
    head_out = head_out.reshape(head_out.shape[0], -1)
    return layer_call(
        head_out,
        residual_in.T,
        norm_gain.reshape(1, OWN),
        expert_ids.T,
        gate_vals.T,
        w_out.T,
        w_gate.reshape(2, 8, OWN, 256),
        w_up.reshape(2, 8, OWN, 256),
        w_down[0],
    ).T


def solution(mesh):
    placed = (
        P(("side", "row"), "col", None),
        P(("side", "row"), None, None),
        P(("side", "row")),
        P("col", None, None),
        P("col", ("side", "row")),
        P("col", ("side", "row")),
        P(("side", "row")),
        P("col", None),
        P("col", None),
        P(("side", "row"), None, "col"),
        P(("side", "row"), None, "col"),
        P(("side", "row"), "col", None),
    )
    return jax.shard_map(
        shards, mesh=mesh, in_specs=placed, out_specs=P("col", ("side", "row")), check_vma=False
    )
```

```python
import jax
import jax.numpy as jnp
from jax import lax
from jax.experimental import pallas as pl
from jax.experimental.pallas import tpu as pltpu
from jax.sharding import PartitionSpec as P

D = 7168
ROPE = 64
HD = 128
HALF = 64
OWN = 448
PAIR = 896
MESH = pl.DeviceIdType.MESH
BF16 = jnp.bfloat16
F32 = jnp.float32

LANES = ((0, 384), (384, 256), (640, 256))
ORDERS = (
    (("x", "y", "z"), ("y", "z", "x"), ("z", "x", "y")),
    (("y", "z", "x"), ("z", "x", "y"), ("x", "y", "z")),
)
HEAD_LANES = ((0, 1152), (1152, 896))
SUM_LANES = ((0, 512), (512, 384))
LOW, HIGH, ALL = (0, 32), (32, 32), (0, 64)
DIRECT_GATHERS = ((0, 0), (1, 0), (0, 1))
DIRECT_SCATTERS = ((0, 2), (1, 1), (1, 2))
GROUP = 8


class Place:
    def __init__(self):
        self.side, self.row, self.col = (lax.axis_index(name) for name in ("side", "row", "col"))
        z_hi, y = lax.div(self.row, 4), lax.rem(self.row, 4)
        z_lo, x = lax.div(self.col, 4), lax.rem(self.col, 4)
        at = {"x": x, "y": y, "z": z_hi * 2 + z_lo}
        self.coord = {a: [at[a]] + [lax.rem(at[a] + k, 4) for k in (1, 2, 3)] for a in "xyz"}
        self.bits = {a: [(lax.div(j, 2), lax.rem(j, 2)) for j in self.coord[a]] for a in "xyz"}
        self.sibling = (1 - self.side, self.row, self.col)
        self.ids = {"x": [], "y": [], "z": []}
        for k in range(4):
            high, low = self.bits["z"][k]
            self.ids["x"].append((self.side, self.row, z_lo * 4 + self.coord["x"][k]))
            self.ids["y"].append((self.side, z_hi * 4 + self.coord["y"][k], self.col))
            self.ids["z"].append((self.side, high * 4 + y, low * 4 + x))

    def view(self, ref, at, rows, lanes, lead=()):
        index = [slice(None)] * 6
        if "x" in at:
            index[1], index[2] = self.bits["x"][at["x"]]
        if "y" in at:
            index[4], index[5] = self.bits["y"][at["y"]]
        if "z" in at:
            index[3], index[0] = self.bits["z"][at["z"]]
        return ref.at[(*lead, *index, pl.ds(*rows), pl.ds(*lanes))]


def remote(src, dst, send_sem, recv_sem, device):
    return pltpu.make_async_remote_copy(
        src_ref=src,
        dst_ref=dst,
        send_sem=send_sem,
        recv_sem=recv_sem,
        device_id=device,
        device_id_type=MESH,
    )


class RingGather:
    def __init__(self, here, axis, bundle, halves, sems):
        self.here, self.axis, self.bundle, self.halves, self.sems = here, axis, bundle, halves, sems

    def copy(self, direction, piece):
        send, recv = self.sems
        up = (1, 3)[direction]
        half = self.halves[direction if piece != 1 else 1 - direction]
        ref = self.bundle(0 if piece < 2 else 4 - up, half)
        device = self.here.ids[self.axis][up]
        return remote(ref, ref, send.at[direction, piece], recv.at[direction, piece], device)

    def start(self):
        for piece in range(2):
            for direction in range(2):
                self.copy(direction, piece).start()

    def relay(self):
        for direction in range(2):
            self.copy(direction, 0).wait_recv()
            self.copy(direction, 2).start()

    def near(self):
        for direction in range(2):
            self.copy(direction, 1).wait_recv()

    def far(self):
        for direction in range(2):
            self.copy(direction, 2).wait_recv()

    def drain(self):
        for direction in range(2):
            for piece in range(3):
                self.copy(direction, piece).wait_send()


class RingScatter:
    def __init__(self, here, axis, bundle, halves, arrived, sems):
        self.here, self.axis, self.bundle, self.halves = here, axis, bundle, halves
        self.arrived, self.sems = arrived, sems

    def place(self, direction, piece):
        k = 2 if piece == 0 else (1, 3)[direction]
        return self.bundle(k, self.halves[direction if piece != 1 else 1 - direction])

    def copy(self, direction, piece):
        send, recv = self.sems
        return remote(
            self.place(direction, piece),
            self.arrived.at[direction, piece],
            send.at[direction, piece],
            recv.at[direction, piece],
            self.here.ids[self.axis][(1, 3)[direction]],
        )

    def start(self):
        for piece in range(2):
            for direction in range(2):
                self.copy(direction, piece).start()

    def relay(self):
        for direction in range(2):
            self.copy(direction, 0).wait_recv()
            target = self.place(direction, 2)
            target[...] = (target[...].astype(F32) + self.arrived[direction, 0].astype(F32)).astype(BF16)
            self.copy(direction, 2).start()

    def finish(self, use=None):
        for direction in range(2):
            self.copy(direction, 1).wait_recv()
            self.copy(direction, 2).wait_recv()
        for rows, (first, second) in zip(self.halves, ((2, 1), (1, 2))):
            target = self.bundle(0, rows)
            value = target[...].astype(F32) + (
                self.arrived[0, first].astype(F32) + self.arrived[1, second].astype(F32)
            )
            if use is None:
                target[...] = value.astype(BF16)
            else:
                use(rows, value)

    def drain(self):
        for direction in range(2):
            for piece in range(3):
                self.copy(direction, piece).wait_send()


class DirectGather:
    def __init__(self, here, axis, bundle, halves, sems):
        self.here, self.axis, self.bundle, self.sems = here, axis, bundle, sems
        self.rows = (halves[0][0], 2 * halves[0][1])

    def copies(self):
        send, recv = self.sems
        ref = self.bundle(0, self.rows)
        for k in (2, 1, 3):
            yield remote(ref, ref, send.at[0, k - 1], recv.at[0, k - 1], self.here.ids[self.axis][k])

    def start(self):
        for copy in self.copies():
            copy.start()

    def far(self):
        for copy in self.copies():
            copy.wait_recv()

    def drain(self):
        for copy in self.copies():
            copy.wait_send()


class DirectScatter:
    def __init__(self, here, axis, bundle, halves, arrived, sems):
        self.here, self.axis, self.bundle, self.arrived, self.sems = here, axis, bundle, arrived, sems
        self.rows = (halves[0][0], 2 * halves[0][1])

    def copies(self):
        send, recv = self.sems
        for k in (2, 1, 3):
            yield remote(
                self.bundle(k, self.rows),
                self.arrived.at[k - 1],
                send.at[0, k - 1],
                recv.at[0, k - 1],
                self.here.ids[self.axis][k],
            )

    def start(self):
        for copy in self.copies():
            copy.start()

    def finish(self, use=None):
        for copy in self.copies():
            copy.wait_recv()
        target = self.bundle(0, self.rows)
        value = target[...].astype(F32) + (
            self.arrived[0].astype(F32) + (self.arrived[1].astype(F32) + self.arrived[2].astype(F32))
        )
        if use is None:
            target[...] = value.astype(BF16)
        else:
            use(self.rows, value)

    def drain(self):
        for copy in self.copies():
            copy.wait_send()


def layer_kernel(
    head_ref, residual_ref, gain_ref, ids_ref, vals_ref, out_hbm, gate_hbm, up_hbm, down_hbm, out_ref,
    heads, proj, part_sums, z_early, z_late, x_early, x_late, pair, pair_sib, pair_all, hidden, square,
    rows_buf, weights, down, down_pairs, total, acts, squares, inverses, gates, columns,
    from_sibling, mixed, mixed_sib,
    load_sems, head_sems, flip_sems, sum_sems, pair_sems, proj_sems, small_send, small_recv,
    send_sems, recv_sems, share_send, share_recv, back_send, back_recv, last_sems, *arrivals,
):
    here = Place()
    side, row, col, sibling = here.side, here.row, here.col, here.sibling
    (z_hi, z_lo), (x_hi, x_lo), (y_hi, y_lo) = (here.bits[axis][0] for axis in "zxy")
    x = here.coord["x"][0]
    far_z = here.ids["z"][2]
    flip_z = (side, row, lax.rem(col + 4, 8))

    def row_peer(k):
        return (side, lax.rem(row + k, 8), col)

    def col_peer(k):
        return (side, row, lax.rem(col + k, 8))


    loads = [
        pltpu.make_async_copy(
            source.at[core],
            weights.at[:, core, :, pl.ds(which * 256, 256)],
            load_sems.at[which * 2 + core],
        )
        for which, source in enumerate((gate_hbm, up_hbm))
        for core in range(2)
    ]
    load_proj = pltpu.make_async_copy(out_hbm, proj.at[side], load_sems.at[4])
    load_down = pltpu.make_async_copy(down_hbm, down, load_sems.at[5])
    heads[side, z_hi, y_hi, y_lo] = head_ref[...]

    barrier = pltpu.get_barrier_semaphore()
    peers = [sibling, *map(row_peer, range(1, 8)), *map(col_peer, range(1, 8)), here.ids["z"][1], here.ids["z"][3]]
    for peer in peers:
        pl.semaphore_signal(barrier, inc=1, device_id=peer, device_id_type=MESH)
    pl.semaphore_wait(barrier, len(peers))

    def head_view(which, at, rows):
        return heads.at[(side, *at, pl.ds(*rows), pl.ds(*HEAD_LANES[which]))]

    def head_ring(index, which, z):
        return RingGather(
            here,
            "y",
            lambda k, rows: head_view(which, (z, *here.bits["y"][k]), rows),
            (LOW, HIGH),
            (head_sems.at[0, index], head_sems.at[1, index]),
        )

    def head_flip(index, which, k):
        ref = head_view(which, (z_hi, *here.bits["y"][k]), ALL)
        return remote(ref, ref, flip_sems.at[0, index], flip_sems.at[1, index], far_z)

    flips = [head_flip(0, 0, 0)] + [head_flip(1 + k, 1, k) for k in range(4)]
    rings = [head_ring(0, 1, z_hi), head_ring(1, 0, z_hi), head_ring(2, 0, 1 - z_hi)]
    flips[0].start()
    rings[0].start()
    rings[1].start()
    flips[1].start()
    load_proj.start()
    for load in loads:
        load.start()
    load_down.start()

    owner = side * 8 + row
    chosen = jnp.where(ids_ref[...] == owner, vals_ref[...], 0.0)
    gates[col] = jnp.broadcast_to(jnp.sum(chosen, axis=0, keepdims=True), (8, 128))
    square[0:OWN] = residual_ref[...].astype(F32)
    square[OWN:512] = jnp.zeros((512 - OWN, 128), F32)
    residual = square[...].T.astype(BF16)
    for half in range(2):
        pair[half, 0:HALF] = residual[half * HALF : (half + 1) * HALF, 0:OWN]
        pair[half, HALF:80] = jnp.broadcast_to(gain_ref[...].astype(F32), (16, OWN)).astype(BF16)
    pair_copy = remote(pair.at[1 - side], pair_sib, pair_sems.at[0], pair_sems.at[1], sibling)
    pair_copy.start()
    proj_copy = remote(out_hbm, proj.at[side], proj_sems.at[0], proj_sems.at[1], sibling)
    proj_copy.start()
    def smalls(kind, ref, name):
        @pl.loop(0, 7)
        def _(k):
            peer = row_peer(k + 1) if kind == 1 else col_peer(k + 1)
            getattr(remote(ref, ref, small_send.at[kind, k], small_recv.at[kind, k], peer), name)()

    smalls(0, gates.at[col], "start")

    rings[0].relay()
    flips[0].wait_recv()
    rings[2].start()
    rings[0].near()
    flips[2].start()
    flips[4].start()
    rings[1].relay()
    rings[0].far()
    flips[3].start()

    pair_copy.wait_recv()

    @pl.when(side == 0)
    def _():
        pair_all[:, 0:OWN] = pair[0]
        pair_all[:, OWN:PAIR] = pair_sib[...]

    @pl.when(side == 1)
    def _():
        pair_all[:, 0:OWN] = pair_sib[...]
        pair_all[:, OWN:PAIR] = pair[1]

    rings[2].relay()
    for ring in rings[1:]:
        ring.near()
        ring.far()
    for flip in flips[1:]:
        flip.wait_recv()
    theirs = heads.at[side, :, :, 1 - side]
    head_share = remote(theirs, theirs, pair_sems.at[2], pair_sems.at[3], sibling)
    head_share.start()

    load_proj.wait()
    proj_copy.wait_recv()

    def project(source):
        lhs = heads[source, :, :, side].reshape(4 * HALF, 2048)
        value = lax.dot_general(
            lhs, proj[...].reshape(PAIR, 2048), (((1,), (1,)), ((), ())), preferred_element_type=F32
        )
        part_sums[source] = value.astype(BF16).reshape(4, HALF, PAIR)

    project(side)
    head_share.wait_recv()
    project(1 - side)

    def x_ring(kind, which, lead, arrived):
        return kind(
            here,
            "x",
            lambda k, rows: part_sums.at[lead, here.coord["x"][k], pl.ds(*rows), pl.ds(*SUM_LANES[which])],
            (LOW, HIGH),
            arrived,
            (sum_sems.at[0, which], sum_sems.at[1, which]),
        )

    early_flip = remote(
        part_sums.at[1 - z_lo, :, :, pl.ds(*SUM_LANES[1])], z_early, flip_sems.at[0, 5], flip_sems.at[1, 5], flip_z
    )
    early_flip.start()
    early_ring = x_ring(RingScatter, 0, slice(None), x_early)
    early_ring.start()
    early_ring.relay()
    early_flip.wait_recv()
    mine = part_sums.at[z_lo, :, :, pl.ds(*SUM_LANES[1])]
    mine[...] = (mine[...].astype(F32) + z_early[...].astype(F32)).astype(BF16)
    late_ring = x_ring(DirectScatter, 1, z_lo, x_late)
    late_ring.start()
    early_ring.finish()
    late_flip = remote(
        part_sums.at[1 - z_lo, x, :, pl.ds(*SUM_LANES[0])], z_late, flip_sems.at[0, 6], flip_sems.at[1, 6], flip_z
    )
    late_flip.start()
    late_flip.wait_recv()
    left = pl.ds(*SUM_LANES[0])
    hidden[:, left] = pair_all[0:HALF, left].astype(F32) + (
        part_sums[z_lo, x, :, left].astype(F32) + z_late[...].astype(F32)
    )

    def right(rows, value):
        spot = (pl.ds(*rows), pl.ds(*SUM_LANES[1]))
        hidden[spot] = pair_all[spot].astype(F32) + value

    late_ring.finish(right)
    rows_buf[side, z_lo, x_hi, x_lo, z_hi, y_hi, y_lo] = (
        hidden[...] * pair_all[HALF : HALF + 1].astype(F32)
    ).astype(BF16)

    def per_core(step):
        for core in range(2):

            @pl.when(side == core)
            def _(core=core):
                step(ORDERS[core])

    def halves(t):
        return (t * 32, 16), (t * 32 + 16, 16)

    def gather_rings(t, phase, orders):
        for part in range(3):
            axis = orders[part][phase]
            own = {a: 0 for a in orders[part][phase:]}
            yield (DirectGather if (t, phase) in DIRECT_GATHERS else RingGather)(
                here,
                axis,
                lambda k, rows, part=part, own=own, axis=axis: here.view(
                    rows_buf, {**own, axis: k}, rows, LANES[part], (side,)
                ),
                halves(t),
                (send_sems.at[0, t, part, phase], recv_sems.at[0, t, part, phase]),
            )

    def scatter_rings(t, phase, orders):
        for part in range(3):
            axis = orders[part][phase]
            done = {a: 0 for a in orders[part][:phase]}
            yield (DirectScatter if (t, phase) in DIRECT_SCATTERS else RingScatter)(
                here,
                axis,
                lambda k, rows, part=part, done=done, axis=axis: here.view(
                    rows_buf, {**done, axis: k}, rows, LANES[part], (side,)
                ),
                halves(t),
                arrivals[(t * 3 + phase) * 3 + part],
                (send_sems.at[1, t, part, phase], recv_sems.at[1, t, part, phase]),
            )

    def each(rings, *names):
        def step(orders):
            made = list(rings(orders))
            for name in names:
                for ring in made:
                    getattr(ring, name)()

        per_core(step)

    def gather(t, phase, *names):
        each(lambda orders: gather_rings(t, phase, orders), *names)

    def scatter(t, phase, *names):
        each(lambda orders: scatter_rings(t, phase, orders), *names)

    def share(t, part, k, orders):
        ref = here.view(rows_buf, {orders[part][2]: k}, (t * 32, 32), LANES[part], (side,))
        return remote(ref, ref, share_send.at[t, part, k], share_recv.at[t, part, k], sibling)

    def shares(t, steps, name):
        def step(orders):
            for part in range(3):
                for k in steps:
                    getattr(share(t, part, k, orders), name)()

        per_core(step)

    def chunk(r):
        return lax.div(r, 4), lax.rem(lax.div(r, 2), 2), lax.rem(r, 2)

    def back(t, r):
        return remote(
            rows_buf.at[(1 - side,) + (slice(None),) * 3 + chunk(r) + (pl.ds(t * 32, 32),)],
            from_sibling.at[t, r],
            back_send.at[t, r],
            back_recv.at[t, r],
            sibling,
        )

    def experts(t, half, place):
        total[...] = jnp.zeros_like(total)

        @pl.loop(0, 8)
        def _(r):
            lhs = rows_buf[(half,) + (slice(None),) * 3 + chunk(r) + (pl.ds(t * 32, 32),)].reshape(256, PAIR)
            total[...] += jnp.dot(lhs, weights[r].reshape(PAIR, 512), preferred_element_type=F32)

        gate_rows = columns[pl.ds(pl.multiple_of(half * HALF + t * 32, 32), 32)]
        for c in range(8):
            first = c * 32
            scale = columns[t * 32 : t * 32 + 32, place + c : place + c + 1]
            gate_part = total[first : first + 32, :256] * scale
            up_part = total[first : first + 32, 256:] * (scale * gate_rows[:, c : c + 1])
            acts[half, first : first + 32] = (gate_part / (1.0 + jnp.exp(-gate_part)) * up_part).astype(BF16)

    def down_theirs(t):
        @pl.loop(0, 8)
        def _(r):
            value = jnp.dot(acts[1 - side], down_pairs[r], preferred_element_type=F32).astype(BF16)
            rows_buf[(1 - side,) + (slice(None),) * 3 + chunk(r) + (pl.ds(t * 32, 32),)] = value.reshape(2, 2, 2, 32, PAIR)
            back(t, r).start()

    def down_own(t):
        @pl.loop(0, 8)
        def _(r):
            value = jnp.dot(acts[side], down_pairs[r], preferred_element_type=F32)
            back(t, r).wait_recv()
            value = value + from_sibling[t, r].reshape(256, PAIR).astype(F32)
            rows_buf[(side,) + (slice(None),) * 3 + chunk(r) + (pl.ds(t * 32, 32),)] = value.astype(BF16).reshape(
                2, 2, 2, 32, PAIR
            )

    def final(t):
        def step(orders):
            for part, ring in enumerate(scatter_rings(t, 2, orders)):

                def use(rows, value, part=part):
                    spot = (pl.ds(*rows), pl.ds(*LANES[part]))
                    mixed[spot] = (hidden[spot] + value).astype(BF16)

                ring.finish(use)

        per_core(step)

    def experts_own(t):
        experts(t, side, 8)

    def experts_theirs(t):
        experts(t, 1 - side, 16)

    def last(t):
        rows = pl.ds(t * 32, 32)
        return remote(mixed.at[rows], mixed_sib.at[rows], last_sems.at[0, t], last_sems.at[1, t], sibling)

    gather(0, 0, "start")
    gather(1, 0, "start")
    value = hidden[...]
    columns[0:HALF] = jnp.broadcast_to(jnp.sum(value * value, axis=1, keepdims=True), (HALF, 128))
    columns[HALF:128] = jnp.zeros((HALF, 128), F32)
    squares[row] = columns[...].T[0:8]
    smalls(1, squares.at[row], "start")
    gather(0, 0, "far")
    gather(0, 1, "start")
    gather(1, 0, "far")
    gather(1, 1, "start")
    smalls(1, squares.at[row], "wait_recv")
    inverses[side, col] = lax.rsqrt(jnp.sum(squares[...], axis=0) / D + 1e-06)
    smalls(2, inverses.at[side, col], "start")
    gather(0, 1, "far")
    gather(0, 2, "start")
    shares(0, (0,), "start")
    gather(1, 1, "relay")
    gather(1, 1, "near", "far")
    smalls(2, inverses.at[side, col], "wait_recv")
    inverse_share = remote(
        inverses.at[side], inverses.at[side], pair_sems.at[4], pair_sems.at[5], sibling
    )
    inverse_share.start()
    load_down.wait()
    for r in range(8):
        for core in range(2):
            down_pairs[r, :, core * OWN : (core + 1) * OWN] = down[
                :, (core * 8 + r) * OWN : (core * 8 + r + 1) * OWN
            ]
    gather(0, 2, "relay")
    gather(1, 2, "start")
    shares(1, (0,), "start")
    gather(0, 2, "near")
    shares(0, (1, 3), "start")
    smalls(0, gates.at[col], "wait_recv")
    inverse_share.wait_recv()
    columns[...] = jnp.zeros_like(columns)
    for c in range(8):
        columns[c : c + 1] = gates[c, 0:1]
        columns[8 + c : 9 + c] = inverses[side, c, 0:1]
        columns[16 + c : 17 + c] = inverses[1 - side, c, 0:1]
    columns[...] = columns[...].T
    for load in loads:
        load.wait()
    gather(0, 2, "far")
    shares(0, (2,), "start")
    gather(1, 2, "relay")
    experts_own(0)
    shares(0, (0, 1, 2, 3), "wait_recv")
    experts_theirs(0)
    down_theirs(0)
    gather(1, 2, "near")
    shares(1, (1, 3), "start")
    for phase in range(3):
        gather(0, phase, "drain")
    shares(0, (0, 1, 2, 3), "wait_send")
    down_own(0)
    scatter(0, 0, "start")
    gather(1, 2, "far")
    shares(1, (2,), "start")
    experts_own(1)
    shares(1, (0, 1, 2, 3), "wait_recv")
    experts_theirs(1)
    down_theirs(1)
    scatter(0, 0, "relay")
    for phase in range(3):
        gather(1, phase, "drain")
    shares(1, (0, 1, 2, 3), "wait_send")
    down_own(1)
    scatter(1, 0, "start")
    scatter(0, 0, "finish")
    scatter(0, 1, "start")
    scatter(1, 0, "relay")
    scatter(0, 1, "relay")
    scatter(0, 1, "finish")
    scatter(0, 2, "start")
    final(0)
    last(0).start()
    scatter(1, 0, "finish")
    scatter(1, 1, "start")
    scatter(1, 1, "finish")
    scatter(1, 2, "start")
    final(1)
    last(1).start()
    for t in range(2):
        last(t).wait_recv()

    def transposed(top, bottom):
        square[0:PAIR // 2, 0:HALF] = top.astype(F32).T
        square[0:PAIR // 2, HALF:128] = bottom.astype(F32).T
        out_ref[...] = square[0:OWN].astype(BF16)

    @pl.when(side == 0)
    def _():
        transposed(mixed[:, 0:OWN], mixed_sib[:, 0:OWN])

    @pl.when(side == 1)
    def _():
        transposed(mixed_sib[:, OWN:PAIR], mixed[:, OWN:PAIR])

    for t in range(2):
        last(t).wait_send()
    for ring in (*rings, early_ring, late_ring):
        ring.drain()
    for copy in (
        *flips, early_flip, late_flip, pair_copy, proj_copy, head_share, inverse_share,
    ):
        copy.wait_send()
    smalls(0, gates.at[col], "wait_send")
    smalls(1, squares.at[row], "wait_send")
    smalls(2, inverses.at[side, col], "wait_send")
    for t in range(2):
        for phase in range(3):
            scatter(t, phase, "drain")

        @pl.loop(0, 8)
        def _(r, t=t):
            back(t, r).wait_send()


ARRIVALS = [
    (
        *((3,) if (t, phase) in DIRECT_SCATTERS else (2, 3)),
        *(2,) * (4 - 2 * phase),
        32 if (t, phase) in DIRECT_SCATTERS else 16,
        LANES[part][1],
    )
    for t in range(2)
    for phase in range(3)
    for part in range(3)
]

VMEM = pl.BlockSpec(memory_space=pltpu.VMEM)
ANY = pl.BlockSpec(memory_space=pl.ANY)
DMA = pltpu.SemaphoreType.DMA


def attend_kernel(lengths_ref, queries_ref, cache_ref, up_ref, out_ref, latent):
    step = pl.program_id(0)
    lane = lax.broadcasted_iota(jnp.int32, (16, 128), 1)
    scores = []
    for i in range(GROUP):
        score = jnp.dot(queries_ref[i], cache_ref[i], preferred_element_type=F32) * (HD + ROPE) ** (-0.5)
        scores.append(jnp.where(lane < lengths_ref[step * GROUP + i], score, -jnp.inf))
    scores = jnp.concatenate(scores, axis=0)
    terms = jnp.exp(scores - jnp.max(scores, axis=1, keepdims=True))
    probs = (terms / jnp.sum(terms, axis=1, keepdims=True)).astype(BF16)
    for i in range(GROUP):
        value = lax.dot_general(
            probs[i * 16 : (i + 1) * 16],
            cache_ref[i, 0:512],
            (((1,), (1,)), ((), ())),
            preferred_element_type=F32,
        )
        for k in range(4):
            latent[k, pl.ds(pl.multiple_of((step * GROUP + i) * 16, 16), 16)] = value[:, k * 128 : k * 128 + 128]

    @pl.when(step == HALF // GROUP - 1)
    def _():
        for head in range(16):
            rows = jnp.concatenate(
                [latent[k, pl.ds(head, HALF, stride=16)] for k in range(4)], axis=1
            ).astype(BF16)
            out_ref[:, head * HD : (head + 1) * HD] = jnp.dot(
                rows, up_ref[head], preferred_element_type=F32
            ).astype(BF16)


def attend_call(lengths, queries, cache, w_uv):
    return pl.pallas_call(
        attend_kernel,
        out_shape=jax.ShapeDtypeStruct((HALF, 16 * HD), BF16),
        grid=(HALF // GROUP,),
        in_specs=[
            pl.BlockSpec(memory_space=pltpu.SMEM),
            pl.BlockSpec((GROUP, 16, 576), lambda i: (i, 0, 0)),
            pl.BlockSpec((GROUP, 576, 128), lambda i: (i, 0, 0)),
            pl.BlockSpec((16, 512, HD), lambda i: (0, 0, 0)),
        ],
        out_specs=pl.BlockSpec((HALF, 16 * HD), lambda i: (0, 0)),
        scratch_shapes=[pltpu.VMEM((4, HALF * 16, 128), F32)],
        compiler_params=pltpu.CompilerParams(vmem_limit_bytes=58 * 2**20),
        cost_estimate=pl.CostEstimate(
            flops=2 * 64 * 16 * 128 * 1700, bytes_accessed=14 * 2**20, transcendentals=2**17
        ),
    )(lengths, queries, cache, w_uv)


def layer_call(*args):
    scratch = [
        pltpu.VMEM((2, 2, 2, 2, HALF, 2048), BF16),
        pltpu.VMEM((2, OWN, 2048), BF16),
        pltpu.VMEM((2, 4, HALF, PAIR), BF16),
        pltpu.VMEM((4, HALF, SUM_LANES[1][1]), BF16),
        pltpu.VMEM((HALF, SUM_LANES[0][1]), BF16),
        pltpu.VMEM((2, 3, 2, 32, SUM_LANES[0][1]), BF16),
        pltpu.VMEM((3, HALF, SUM_LANES[1][1]), BF16),
        pltpu.VMEM((2, 80, OWN), BF16),
        pltpu.VMEM((80, OWN), BF16),
        pltpu.VMEM((80, PAIR), BF16),
        pltpu.VMEM((HALF, PAIR), F32),
        pltpu.VMEM((512, 128), F32),
        pltpu.VMEM((2, 2, 2, 2, 2, 2, 2, HALF, PAIR), BF16),
        pltpu.VMEM((8, 2, OWN, 512), BF16),
        pltpu.VMEM((256, D), BF16),
        pltpu.VMEM((8, 256, PAIR), BF16),
        pltpu.VMEM((256, 512), F32),
        pltpu.VMEM((2, 256, 256), BF16),
        pltpu.VMEM((8, 8, 128), F32),
        pltpu.VMEM((2, 8, 8, 128), F32),
        pltpu.VMEM((8, 8, 128), F32),
        pltpu.VMEM((128, 128), F32),
        pltpu.VMEM((2, 8, 2, 2, 2, 32, PAIR), BF16),
        pltpu.VMEM((HALF, PAIR), BF16),
        pltpu.VMEM((HALF, PAIR), BF16),
        DMA((6,)),
        DMA((2, 3, 2, 3)),
        DMA((2, 7)),
        DMA((2, 2, 2, 3)),
        DMA((8,)),
        DMA((2,)),
        DMA((3, 7)),
        DMA((3, 7)),
        DMA((2, 2, 3, 3, 2, 3)),
        DMA((2, 2, 3, 3, 2, 3)),
        DMA((2, 3, 4)),
        DMA((2, 3, 4)),
        DMA((2, 8)),
        DMA((2, 8)),
        DMA((2, 2)),
        *[pltpu.VMEM(shape, BF16) for shape in ARRIVALS],
    ]
    return pl.pallas_call(
        layer_kernel,
        out_shape=jax.ShapeDtypeStruct((OWN, 2 * HALF), BF16),
        in_specs=[VMEM] * 5 + [ANY] * 4,
        out_specs=VMEM,
        scratch_shapes=scratch,
        compiler_params=pltpu.CompilerParams(
            collective_id=0, has_side_effects=True, vmem_limit_bytes=58 * 2**20
        ),
        cost_estimate=pl.CostEstimate(
            flops=2 * 1024 * 7168 * 1000, bytes_accessed=16 * 2**20, transcendentals=2**18
        ),
    )(*args)


def shards(
    queries,
    cache,
    lengths,
    w_uv,
    w_out,
    residual_in,
    norm_gain,
    expert_ids,
    gate_vals,
    w_gate,
    w_up,
    w_down,
):
    head_out = attend_call(lengths, queries, cache.swapaxes(1, 2), w_uv)
    return layer_call(
        head_out,
        residual_in.T,
        norm_gain.reshape(1, OWN),
        expert_ids.T,
        gate_vals.T,
        w_out.T,
        w_gate.reshape(2, 8, OWN, 256),
        w_up.reshape(2, 8, OWN, 256),
        w_down[0],
    ).T


def solution(mesh):
    placed = (
        P(("side", "row"), "col", None),
        P(("side", "row"), None, None),
        P(("side", "row")),
        P("col", None, None),
        P("col", ("side", "row")),
        P("col", ("side", "row")),
        P(("side", "row")),
        P("col", None),
        P("col", None),
        P(("side", "row"), None, "col"),
        P(("side", "row"), None, "col"),
        P(("side", "row"), "col", None),
    )
    return jax.shard_map(
        shards, mesh=mesh, in_specs=placed, out_specs=P("col", ("side", "row")), check_vma=False
    )
```

```python
import jax
import jax.numpy as jnp
from jax import lax
from jax.experimental import pallas as pl
from jax.experimental.pallas import tpu as pltpu
from jax.sharding import PartitionSpec as P

D = 7168
ROPE = 64
HD = 128
HALF = 64
OWN = 448
PAIR = 896
MESH = pl.DeviceIdType.MESH
BF16 = jnp.bfloat16
F32 = jnp.float32

LANES = ((0, 384), (384, 256), (640, 256))
ORDERS = (
    (("x", "y", "z"), ("y", "z", "x"), ("z", "x", "y")),
    (("y", "z", "x"), ("z", "x", "y"), ("x", "y", "z")),
)
HEAD_LANES = ((0, 1152), (1152, 896))
SUM_LANES = ((0, 512), (512, 384))
LOW, HIGH, ALL = (0, 32), (32, 32), (0, 64)
DIRECT_GATHERS = ((0, 0), (1, 0), (0, 1))
DIRECT_SCATTERS = ((0, 2), (1, 1), (1, 2))
GROUP = 8


class Place:
    def __init__(self):
        self.side, self.row, self.col = (lax.axis_index(name) for name in ("side", "row", "col"))
        z_hi, y = lax.div(self.row, 4), lax.rem(self.row, 4)
        z_lo, x = lax.div(self.col, 4), lax.rem(self.col, 4)
        at = {"x": x, "y": y, "z": z_hi * 2 + z_lo}
        self.coord = {a: [at[a]] + [lax.rem(at[a] + k, 4) for k in (1, 2, 3)] for a in "xyz"}
        self.bits = {a: [(lax.div(j, 2), lax.rem(j, 2)) for j in self.coord[a]] for a in "xyz"}
        self.sibling = (1 - self.side, self.row, self.col)
        self.ids = {"x": [], "y": [], "z": []}
        for k in range(4):
            high, low = self.bits["z"][k]
            self.ids["x"].append((self.side, self.row, z_lo * 4 + self.coord["x"][k]))
            self.ids["y"].append((self.side, z_hi * 4 + self.coord["y"][k], self.col))
            self.ids["z"].append((self.side, high * 4 + y, low * 4 + x))

    def view(self, ref, at, rows, lanes, lead=()):
        index = [slice(None)] * 6
        if "x" in at:
            index[1], index[2] = self.bits["x"][at["x"]]
        if "y" in at:
            index[4], index[5] = self.bits["y"][at["y"]]
        if "z" in at:
            index[3], index[0] = self.bits["z"][at["z"]]
        return ref.at[(*lead, *index, pl.ds(*rows), pl.ds(*lanes))]


def remote(src, dst, send_sem, recv_sem, device):
    return pltpu.make_async_remote_copy(
        src_ref=src,
        dst_ref=dst,
        send_sem=send_sem,
        recv_sem=recv_sem,
        device_id=device,
        device_id_type=MESH,
    )


class RingGather:
    def __init__(self, here, axis, bundle, halves, sems):
        self.here, self.axis, self.bundle, self.halves, self.sems = here, axis, bundle, halves, sems

    def copy(self, direction, piece):
        send, recv = self.sems
        up = (1, 3)[direction]
        half = self.halves[direction if piece != 1 else 1 - direction]
        ref = self.bundle(0 if piece < 2 else 4 - up, half)
        device = self.here.ids[self.axis][up]
        return remote(ref, ref, send.at[direction, piece], recv.at[direction, piece], device)

    def start(self):
        for piece in range(2):
            for direction in range(2):
                self.copy(direction, piece).start()

    def relay(self):
        for direction in range(2):
            self.copy(direction, 0).wait_recv()
            self.copy(direction, 2).start()

    def near(self):
        for direction in range(2):
            self.copy(direction, 1).wait_recv()

    def far(self):
        for direction in range(2):
            self.copy(direction, 2).wait_recv()

    def drain(self):
        for direction in range(2):
            for piece in range(3):
                self.copy(direction, piece).wait_send()


class RingScatter:
    def __init__(self, here, axis, bundle, halves, arrived, sems):
        self.here, self.axis, self.bundle, self.halves = here, axis, bundle, halves
        self.arrived, self.sems = arrived, sems

    def place(self, direction, piece):
        k = 2 if piece == 0 else (1, 3)[direction]
        return self.bundle(k, self.halves[direction if piece != 1 else 1 - direction])

    def copy(self, direction, piece):
        send, recv = self.sems
        return remote(
            self.place(direction, piece),
            self.arrived.at[direction, piece],
            send.at[direction, piece],
            recv.at[direction, piece],
            self.here.ids[self.axis][(1, 3)[direction]],
        )

    def start(self):
        for piece in range(2):
            for direction in range(2):
                self.copy(direction, piece).start()

    def relay(self):
        for direction in range(2):
            self.copy(direction, 0).wait_recv()
            target = self.place(direction, 2)
            target[...] = (target[...].astype(F32) + self.arrived[direction, 0].astype(F32)).astype(BF16)
            self.copy(direction, 2).start()

    def finish(self, use=None):
        for direction in range(2):
            self.copy(direction, 1).wait_recv()
            self.copy(direction, 2).wait_recv()
        for rows, (first, second) in zip(self.halves, ((2, 1), (1, 2))):
            target = self.bundle(0, rows)
            value = target[...].astype(F32) + (
                self.arrived[0, first].astype(F32) + self.arrived[1, second].astype(F32)
            )
            if use is None:
                target[...] = value.astype(BF16)
            else:
                use(rows, value)

    def drain(self):
        for direction in range(2):
            for piece in range(3):
                self.copy(direction, piece).wait_send()


class DirectGather:
    def __init__(self, here, axis, bundle, halves, sems):
        self.here, self.axis, self.bundle, self.sems = here, axis, bundle, sems
        self.rows = (halves[0][0], 2 * halves[0][1])

    def copies(self):
        send, recv = self.sems
        ref = self.bundle(0, self.rows)
        for k in (2, 1, 3):
            yield remote(ref, ref, send.at[0, k - 1], recv.at[0, k - 1], self.here.ids[self.axis][k])

    def start(self):
        for copy in self.copies():
            copy.start()

    def far(self):
        for copy in self.copies():
            copy.wait_recv()

    def drain(self):
        for copy in self.copies():
            copy.wait_send()


class DirectScatter:
    def __init__(self, here, axis, bundle, halves, arrived, sems):
        self.here, self.axis, self.bundle, self.arrived, self.sems = here, axis, bundle, arrived, sems
        self.rows = (halves[0][0], 2 * halves[0][1])

    def copies(self):
        send, recv = self.sems
        for k in (2, 1, 3):
            yield remote(
                self.bundle(k, self.rows),
                self.arrived.at[k - 1],
                send.at[0, k - 1],
                recv.at[0, k - 1],
                self.here.ids[self.axis][k],
            )

    def start(self):
        for copy in self.copies():
            copy.start()

    def finish(self, use=None):
        for copy in self.copies():
            copy.wait_recv()
        target = self.bundle(0, self.rows)
        value = target[...].astype(F32) + (
            self.arrived[0].astype(F32) + (self.arrived[1].astype(F32) + self.arrived[2].astype(F32))
        )
        if use is None:
            target[...] = value.astype(BF16)
        else:
            use(self.rows, value)

    def drain(self):
        for copy in self.copies():
            copy.wait_send()


def layer_kernel(
    head_ref, residual_ref, gain_ref, ids_ref, vals_ref, out_hbm, gate_hbm, up_hbm, down_hbm, out_ref,
    heads, proj, part_sums, z_early, z_late, x_early, x_late, pair, pair_sib, pair_all, hidden, square,
    rows_buf, weights, down, down_pairs, total, acts, squares, inverses, gates, columns,
    from_sibling, mixed, mixed_sib,
    load_sems, head_sems, flip_sems, sum_sems, pair_sems, proj_sems, small_send, small_recv,
    send_sems, recv_sems, share_send, share_recv, back_send, back_recv, last_sems, *arrivals,
):
    here = Place()
    side, row, col, sibling = here.side, here.row, here.col, here.sibling
    (z_hi, z_lo), (x_hi, x_lo), (y_hi, y_lo) = (here.bits[axis][0] for axis in "zxy")
    x = here.coord["x"][0]
    far_z = here.ids["z"][2]
    flip_z = (side, row, lax.rem(col + 4, 8))

    def row_peer(k):
        return (side, lax.rem(row + k, 8), col)

    def col_peer(k):
        return (side, row, lax.rem(col + k, 8))


    loads = [
        pltpu.make_async_copy(
            source.at[core],
            weights.at[:, core, :, pl.ds(which * 256, 256)],
            load_sems.at[which * 2 + core],
        )
        for which, source in enumerate((gate_hbm, up_hbm))
        for core in range(2)
    ]
    load_proj = pltpu.make_async_copy(out_hbm, proj.at[side], load_sems.at[4])
    load_down = pltpu.make_async_copy(down_hbm, down, load_sems.at[5])
    heads[side, z_hi, y_hi, y_lo] = head_ref[...]

    barrier = pltpu.get_barrier_semaphore()
    peers = [sibling, *map(row_peer, range(1, 8)), *map(col_peer, range(1, 8)), here.ids["z"][1], here.ids["z"][3]]
    for peer in peers:
        pl.semaphore_signal(barrier, inc=1, device_id=peer, device_id_type=MESH)
    pl.semaphore_wait(barrier, len(peers))

    def head_view(which, at, rows):
        return heads.at[(side, *at, pl.ds(*rows), pl.ds(*HEAD_LANES[which]))]

    def head_ring(index, which, z):
        return RingGather(
            here,
            "y",
            lambda k, rows: head_view(which, (z, *here.bits["y"][k]), rows),
            (LOW, HIGH),
            (head_sems.at[0, index], head_sems.at[1, index]),
        )

    def head_flip(index, which, k):
        ref = head_view(which, (z_hi, *here.bits["y"][k]), ALL)
        return remote(ref, ref, flip_sems.at[0, index], flip_sems.at[1, index], far_z)

    flips = [head_flip(0, 0, 0)] + [head_flip(1 + k, 1, k) for k in range(4)]
    rings = [head_ring(0, 1, z_hi), head_ring(1, 0, z_hi), head_ring(2, 0, 1 - z_hi)]
    flips[0].start()
    rings[0].start()
    rings[1].start()
    flips[1].start()
    load_proj.start()
    for load in loads:
        load.start()
    load_down.start()

    owner = side * 8 + row
    chosen = jnp.where(ids_ref[...] == owner, vals_ref[...], 0.0)
    gates[col] = jnp.broadcast_to(jnp.sum(chosen, axis=0, keepdims=True), (8, 128))
    square[0:OWN] = residual_ref[...].astype(F32)
    square[OWN:512] = jnp.zeros((512 - OWN, 128), F32)
    residual = square[...].T.astype(BF16)
    for half in range(2):
        pair[half, 0:HALF] = residual[half * HALF : (half + 1) * HALF, 0:OWN]
        pair[half, HALF:80] = jnp.broadcast_to(gain_ref[...].astype(F32), (16, OWN)).astype(BF16)
    pair_copy = remote(pair.at[1 - side], pair_sib, pair_sems.at[0], pair_sems.at[1], sibling)
    pair_copy.start()
    proj_copy = remote(out_hbm, proj.at[side], proj_sems.at[0], proj_sems.at[1], sibling)
    proj_copy.start()
    def smalls(kind, ref, name):
        @pl.loop(0, 7)
        def _(k):
            peer = row_peer(k + 1) if kind == 1 else col_peer(k + 1)
            getattr(remote(ref, ref, small_send.at[kind, k], small_recv.at[kind, k], peer), name)()

    smalls(0, gates.at[col], "start")

    rings[0].relay()
    flips[0].wait_recv()
    rings[2].start()
    rings[0].near()
    flips[2].start()
    flips[4].start()
    rings[1].relay()
    rings[0].far()
    flips[3].start()

    pair_copy.wait_recv()

    @pl.when(side == 0)
    def _():
        pair_all[:, 0:OWN] = pair[0]
        pair_all[:, OWN:PAIR] = pair_sib[...]

    @pl.when(side == 1)
    def _():
        pair_all[:, 0:OWN] = pair_sib[...]
        pair_all[:, OWN:PAIR] = pair[1]

    rings[2].relay()
    for ring in rings[1:]:
        ring.near()
        ring.far()
    for flip in flips[1:]:
        flip.wait_recv()
    theirs = heads.at[side, :, :, 1 - side]
    head_share = remote(theirs, theirs, pair_sems.at[2], pair_sems.at[3], sibling)
    head_share.start()

    load_proj.wait()
    proj_copy.wait_recv()

    def project(source):
        lhs = heads[source, :, :, side].reshape(4 * HALF, 2048)
        value = lax.dot_general(
            lhs, proj[...].reshape(PAIR, 2048), (((1,), (1,)), ((), ())), preferred_element_type=F32
        )
        part_sums[source] = value.astype(BF16).reshape(4, HALF, PAIR)

    project(side)
    head_share.wait_recv()
    project(1 - side)

    def x_ring(kind, which, lead, arrived):
        return kind(
            here,
            "x",
            lambda k, rows: part_sums.at[lead, here.coord["x"][k], pl.ds(*rows), pl.ds(*SUM_LANES[which])],
            (LOW, HIGH),
            arrived,
            (sum_sems.at[0, which], sum_sems.at[1, which]),
        )

    early_flip = remote(
        part_sums.at[1 - z_lo, :, :, pl.ds(*SUM_LANES[1])], z_early, flip_sems.at[0, 5], flip_sems.at[1, 5], flip_z
    )
    early_flip.start()
    early_ring = x_ring(RingScatter, 0, slice(None), x_early)
    early_ring.start()
    early_ring.relay()
    early_flip.wait_recv()
    mine = part_sums.at[z_lo, :, :, pl.ds(*SUM_LANES[1])]
    mine[...] = (mine[...].astype(F32) + z_early[...].astype(F32)).astype(BF16)
    late_ring = x_ring(DirectScatter, 1, z_lo, x_late)
    late_ring.start()
    early_ring.finish()
    late_flip = remote(
        part_sums.at[1 - z_lo, x, :, pl.ds(*SUM_LANES[0])], z_late, flip_sems.at[0, 6], flip_sems.at[1, 6], flip_z
    )
    late_flip.start()
    late_flip.wait_recv()
    left = pl.ds(*SUM_LANES[0])
    hidden[:, left] = pair_all[0:HALF, left].astype(F32) + (
        part_sums[z_lo, x, :, left].astype(F32) + z_late[...].astype(F32)
    )

    def right(rows, value):
        spot = (pl.ds(*rows), pl.ds(*SUM_LANES[1]))
        hidden[spot] = pair_all[spot].astype(F32) + value

    late_ring.finish(right)
    rows_buf[side, z_lo, x_hi, x_lo, z_hi, y_hi, y_lo] = (
        hidden[...] * pair_all[HALF : HALF + 1].astype(F32)
    ).astype(BF16)

    def per_core(step):
        for core in range(2):

            @pl.when(side == core)
            def _(core=core):
                step(ORDERS[core])

    def halves(t):
        return (t * 32, 16), (t * 32 + 16, 16)

    def gather_rings(t, phase, orders):
        for part in range(3):
            axis = orders[part][phase]
            own = {a: 0 for a in orders[part][phase:]}
            yield (DirectGather if (t, phase) in DIRECT_GATHERS else RingGather)(
                here,
                axis,
                lambda k, rows, part=part, own=own, axis=axis: here.view(
                    rows_buf, {**own, axis: k}, rows, LANES[part], (side,)
                ),
                halves(t),
                (send_sems.at[0, t, part, phase], recv_sems.at[0, t, part, phase]),
            )

    def scatter_rings(t, phase, orders):
        for part in range(3):
            axis = orders[part][phase]
            done = {a: 0 for a in orders[part][:phase]}
            yield (DirectScatter if (t, phase) in DIRECT_SCATTERS else RingScatter)(
                here,
                axis,
                lambda k, rows, part=part, done=done, axis=axis: here.view(
                    rows_buf, {**done, axis: k}, rows, LANES[part], (side,)
                ),
                halves(t),
                arrivals[(t * 3 + phase) * 3 + part],
                (send_sems.at[1, t, part, phase], recv_sems.at[1, t, part, phase]),
            )

    def each(rings, *names):
        def step(orders):
            made = list(rings(orders))
            for name in names:
                for ring in made:
                    getattr(ring, name)()

        per_core(step)

    def gather(t, phase, *names):
        each(lambda orders: gather_rings(t, phase, orders), *names)

    def scatter(t, phase, *names):
        each(lambda orders: scatter_rings(t, phase, orders), *names)

    def share(t, part, k, orders):
        ref = here.view(rows_buf, {orders[part][2]: k}, (t * 32, 32), LANES[part], (side,))
        return remote(ref, ref, share_send.at[t, part, k], share_recv.at[t, part, k], sibling)

    def shares(t, steps, name):
        def step(orders):
            for part in range(3):
                for k in steps:
                    getattr(share(t, part, k, orders), name)()

        per_core(step)

    def chunk(r):
        return lax.div(r, 4), lax.rem(lax.div(r, 2), 2), lax.rem(r, 2)

    def back(t, r):
        return remote(
            rows_buf.at[(1 - side,) + (slice(None),) * 3 + chunk(r) + (pl.ds(t * 32, 32),)],
            from_sibling.at[t, r],
            back_send.at[t, r],
            back_recv.at[t, r],
            sibling,
        )

    def experts(t, half, place):
        total[...] = jnp.zeros_like(total)

        @pl.loop(0, 8)
        def _(r):
            lhs = rows_buf[(half,) + (slice(None),) * 3 + chunk(r) + (pl.ds(t * 32, 32),)].reshape(256, PAIR)
            total[...] += jnp.dot(lhs, weights[r].reshape(PAIR, 512), preferred_element_type=F32)

        gate_rows = columns[pl.ds(pl.multiple_of(half * HALF + t * 32, 32), 32)]
        for c in range(8):
            first = c * 32
            scale = columns[t * 32 : t * 32 + 32, place + c : place + c + 1]
            gate_part = total[first : first + 32, :256] * scale
            up_part = total[first : first + 32, 256:] * (scale * gate_rows[:, c : c + 1])
            acts[half, first : first + 32] = (gate_part / (1.0 + jnp.exp(-gate_part)) * up_part).astype(BF16)

    def down_theirs(t):
        @pl.loop(0, 8)
        def _(r):
            value = jnp.dot(acts[1 - side], down_pairs[r], preferred_element_type=F32).astype(BF16)
            rows_buf[(1 - side,) + (slice(None),) * 3 + chunk(r) + (pl.ds(t * 32, 32),)] = value.reshape(2, 2, 2, 32, PAIR)
            back(t, r).start()

    def down_own(t):
        @pl.loop(0, 8)
        def _(r):
            value = jnp.dot(acts[side], down_pairs[r], preferred_element_type=F32)
            back(t, r).wait_recv()
            value = value + from_sibling[t, r].reshape(256, PAIR).astype(F32)
            rows_buf[(side,) + (slice(None),) * 3 + chunk(r) + (pl.ds(t * 32, 32),)] = value.astype(BF16).reshape(
                2, 2, 2, 32, PAIR
            )

    def final(t):
        def step(orders):
            for part, ring in enumerate(scatter_rings(t, 2, orders)):

                def use(rows, value, part=part):
                    spot = (pl.ds(*rows), pl.ds(*LANES[part]))
                    mixed[spot] = (hidden[spot] + value).astype(BF16)

                ring.finish(use)

        per_core(step)

    def experts_own(t):
        experts(t, side, 8)

    def experts_theirs(t):
        experts(t, 1 - side, 16)

    def last(t):
        rows = pl.ds(t * 32, 32)
        return remote(mixed.at[rows], mixed_sib.at[rows], last_sems.at[0, t], last_sems.at[1, t], sibling)

    gather(0, 0, "start")
    gather(1, 0, "start")
    value = hidden[...]
    columns[0:HALF] = jnp.broadcast_to(jnp.sum(value * value, axis=1, keepdims=True), (HALF, 128))
    columns[HALF:128] = jnp.zeros((HALF, 128), F32)
    squares[row] = columns[...].T[0:8]
    smalls(1, squares.at[row], "start")
    gather(0, 0, "far")
    gather(0, 1, "start")
    gather(1, 0, "far")
    gather(1, 1, "start")
    smalls(1, squares.at[row], "wait_recv")
    inverses[side, col] = lax.rsqrt(jnp.sum(squares[...], axis=0) / D + 1e-06)
    smalls(2, inverses.at[side, col], "start")
    gather(0, 1, "far")
    gather(0, 2, "start")
    shares(0, (0,), "start")
    gather(1, 1, "relay")
    gather(1, 1, "near", "far")
    smalls(2, inverses.at[side, col], "wait_recv")
    inverse_share = remote(
        inverses.at[side], inverses.at[side], pair_sems.at[4], pair_sems.at[5], sibling
    )
    inverse_share.start()
    load_down.wait()
    for r in range(8):
        for core in range(2):
            down_pairs[r, :, core * OWN : (core + 1) * OWN] = down[
                :, (core * 8 + r) * OWN : (core * 8 + r + 1) * OWN
            ]
    smalls(0, gates.at[col], "wait_recv")
    inverse_share.wait_recv()
    columns[...] = jnp.zeros_like(columns)
    for c in range(8):
        columns[c : c + 1] = gates[c, 0:1]
        columns[8 + c : 9 + c] = inverses[side, c, 0:1]
        columns[16 + c : 17 + c] = inverses[1 - side, c, 0:1]
    columns[...] = columns[...].T
    for load in loads:
        load.wait()
    gather(0, 2, "relay")
    gather(0, 2, "near")
    shares(0, (1, 3), "start")
    gather(0, 2, "far")
    gather(1, 2, "start")
    shares(0, (2,), "start")
    shares(1, (0,), "start")
    experts_own(0)
    shares(0, (0, 1, 2, 3), "wait_recv")
    experts_theirs(0)
    down_theirs(0)
    gather(1, 2, "relay")
    for phase in range(3):
        gather(0, phase, "drain")
    shares(0, (0, 1, 2, 3), "wait_send")
    gather(1, 2, "near")
    shares(1, (1, 3), "start")
    down_own(0)
    gather(1, 2, "far")
    shares(1, (2,), "start")
    scatter(0, 0, "start")
    experts_own(1)
    shares(1, (0, 1, 2, 3), "wait_recv")
    experts_theirs(1)
    down_theirs(1)
    scatter(0, 0, "relay")
    for phase in range(3):
        gather(1, phase, "drain")
    shares(1, (0, 1, 2, 3), "wait_send")
    down_own(1)
    scatter(1, 0, "start")
    scatter(0, 0, "finish")
    scatter(0, 1, "start")
    scatter(1, 0, "relay")
    scatter(0, 1, "relay")
    scatter(0, 1, "finish")
    scatter(0, 2, "start")
    final(0)
    last(0).start()
    scatter(1, 0, "finish")
    scatter(1, 1, "start")
    scatter(1, 1, "finish")
    scatter(1, 2, "start")
    final(1)
    last(1).start()
    for t in range(2):
        last(t).wait_recv()

    def transposed(top, bottom):
        square[0:PAIR // 2, 0:HALF] = top.astype(F32).T
        square[0:PAIR // 2, HALF:128] = bottom.astype(F32).T
        out_ref[...] = square[0:OWN].astype(BF16)

    @pl.when(side == 0)
    def _():
        transposed(mixed[:, 0:OWN], mixed_sib[:, 0:OWN])

    @pl.when(side == 1)
    def _():
        transposed(mixed_sib[:, OWN:PAIR], mixed[:, OWN:PAIR])

    for t in range(2):
        last(t).wait_send()
    for ring in (*rings, early_ring, late_ring):
        ring.drain()
    for copy in (
        *flips, early_flip, late_flip, pair_copy, proj_copy, head_share, inverse_share,
    ):
        copy.wait_send()
    smalls(0, gates.at[col], "wait_send")
    smalls(1, squares.at[row], "wait_send")
    smalls(2, inverses.at[side, col], "wait_send")
    for t in range(2):
        for phase in range(3):
            scatter(t, phase, "drain")

        @pl.loop(0, 8)
        def _(r, t=t):
            back(t, r).wait_send()


ARRIVALS = [
    (
        *((3,) if (t, phase) in DIRECT_SCATTERS else (2, 3)),
        *(2,) * (4 - 2 * phase),
        32 if (t, phase) in DIRECT_SCATTERS else 16,
        LANES[part][1],
    )
    for t in range(2)
    for phase in range(3)
    for part in range(3)
]

VMEM = pl.BlockSpec(memory_space=pltpu.VMEM)
ANY = pl.BlockSpec(memory_space=pl.ANY)
DMA = pltpu.SemaphoreType.DMA


def attend_kernel(
    lengths_ref, queries_hbm, cache_hbm, up_hbm, out_ref, queries, cache, up, latent, query_sems, cache_sems, up_sem
):
    def loads(group):
        rows = pl.ds(group * GROUP, GROUP)
        return (
            pltpu.make_async_copy(queries_hbm.at[rows], queries.at[rows], query_sems.at[group]),
            pltpu.make_async_copy(cache_hbm.at[rows], cache.at[rows], cache_sems.at[group]),
        )

    for group in range(HALF // GROUP):
        for load in loads(group):
            load.start()
    load_up = pltpu.make_async_copy(up_hbm, up, up_sem)
    load_up.start()
    lane = lax.broadcasted_iota(jnp.int32, (16, 128), 1)

    @pl.loop(0, HALF // GROUP)
    def _(group):
        for load in loads(group):
            load.wait()
        scores = []
        for i in range(GROUP):
            r = group * GROUP + i
            score = jnp.dot(queries[r], cache[r], preferred_element_type=F32) * (HD + ROPE) ** (-0.5)
            scores.append(jnp.where(lane < lengths_ref[r], score, -jnp.inf))
        scores = jnp.concatenate(scores, axis=0)
        terms = jnp.exp(scores - jnp.max(scores, axis=1, keepdims=True))
        probs = (terms / jnp.sum(terms, axis=1, keepdims=True)).astype(BF16)
        for i in range(GROUP):
            r = group * GROUP + i
            value = lax.dot_general(
                probs[i * 16 : (i + 1) * 16],
                cache[r, 0:512],
                (((1,), (1,)), ((), ())),
                preferred_element_type=F32,
            )
            for k in range(4):
                latent[k, pl.ds(pl.multiple_of(r * 16, 16), 16)] = value[:, k * 128 : k * 128 + 128]

    load_up.wait()
    for head in range(16):
        rows = jnp.concatenate([latent[k, pl.ds(head, HALF, stride=16)] for k in range(4)], axis=1).astype(BF16)
        out_ref[:, head * HD : (head + 1) * HD] = jnp.dot(
            rows, up[head], preferred_element_type=F32
        ).astype(BF16)


def attend_call(lengths, queries, cache, w_uv):
    return pl.pallas_call(
        attend_kernel,
        out_shape=jax.ShapeDtypeStruct((HALF, 16 * HD), BF16),
        in_specs=[pl.BlockSpec(memory_space=pltpu.SMEM), ANY, ANY, ANY],
        out_specs=VMEM,
        scratch_shapes=[
            pltpu.VMEM((HALF, 16, 576), BF16),
            pltpu.VMEM((HALF, 576, 128), BF16),
            pltpu.VMEM((16, 512, HD), BF16),
            pltpu.VMEM((4, HALF * 16, 128), F32),
            pltpu.SemaphoreType.DMA((HALF // GROUP,)),
            pltpu.SemaphoreType.DMA((HALF // GROUP,)),
            pltpu.SemaphoreType.DMA,
        ],
        compiler_params=pltpu.CompilerParams(vmem_limit_bytes=58 * 2**20),
        cost_estimate=pl.CostEstimate(
            flops=2 * 64 * 16 * 128 * 1700, bytes_accessed=14 * 2**20, transcendentals=2**17
        ),
    )(lengths, queries, cache, w_uv)


def layer_call(*args):
    scratch = [
        pltpu.VMEM((2, 2, 2, 2, HALF, 2048), BF16),
        pltpu.VMEM((2, OWN, 2048), BF16),
        pltpu.VMEM((2, 4, HALF, PAIR), BF16),
        pltpu.VMEM((4, HALF, SUM_LANES[1][1]), BF16),
        pltpu.VMEM((HALF, SUM_LANES[0][1]), BF16),
        pltpu.VMEM((2, 3, 2, 32, SUM_LANES[0][1]), BF16),
        pltpu.VMEM((3, HALF, SUM_LANES[1][1]), BF16),
        pltpu.VMEM((2, 80, OWN), BF16),
        pltpu.VMEM((80, OWN), BF16),
        pltpu.VMEM((80, PAIR), BF16),
        pltpu.VMEM((HALF, PAIR), F32),
        pltpu.VMEM((512, 128), F32),
        pltpu.VMEM((2, 2, 2, 2, 2, 2, 2, HALF, PAIR), BF16),
        pltpu.VMEM((8, 2, OWN, 512), BF16),
        pltpu.VMEM((256, D), BF16),
        pltpu.VMEM((8, 256, PAIR), BF16),
        pltpu.VMEM((256, 512), F32),
        pltpu.VMEM((2, 256, 256), BF16),
        pltpu.VMEM((8, 8, 128), F32),
        pltpu.VMEM((2, 8, 8, 128), F32),
        pltpu.VMEM((8, 8, 128), F32),
        pltpu.VMEM((128, 128), F32),
        pltpu.VMEM((2, 8, 2, 2, 2, 32, PAIR), BF16),
        pltpu.VMEM((HALF, PAIR), BF16),
        pltpu.VMEM((HALF, PAIR), BF16),
        DMA((6,)),
        DMA((2, 3, 2, 3)),
        DMA((2, 7)),
        DMA((2, 2, 2, 3)),
        DMA((8,)),
        DMA((2,)),
        DMA((3, 7)),
        DMA((3, 7)),
        DMA((2, 2, 3, 3, 2, 3)),
        DMA((2, 2, 3, 3, 2, 3)),
        DMA((2, 3, 4)),
        DMA((2, 3, 4)),
        DMA((2, 8)),
        DMA((2, 8)),
        DMA((2, 2)),
        *[pltpu.VMEM(shape, BF16) for shape in ARRIVALS],
    ]
    return pl.pallas_call(
        layer_kernel,
        out_shape=jax.ShapeDtypeStruct((OWN, 2 * HALF), BF16),
        in_specs=[VMEM] * 5 + [ANY] * 4,
        out_specs=VMEM,
        scratch_shapes=scratch,
        compiler_params=pltpu.CompilerParams(
            collective_id=0, has_side_effects=True, vmem_limit_bytes=58 * 2**20
        ),
        cost_estimate=pl.CostEstimate(
            flops=2 * 1024 * 7168 * 1000, bytes_accessed=16 * 2**20, transcendentals=2**18
        ),
    )(*args)


def shards(
    queries,
    cache,
    lengths,
    w_uv,
    w_out,
    residual_in,
    norm_gain,
    expert_ids,
    gate_vals,
    w_gate,
    w_up,
    w_down,
):
    head_out = attend_call(lengths, queries, cache.swapaxes(1, 2), w_uv)
    return layer_call(
        head_out,
        residual_in.T,
        norm_gain.reshape(1, OWN),
        expert_ids.T,
        gate_vals.T,
        w_out.T,
        w_gate.reshape(2, 8, OWN, 256),
        w_up.reshape(2, 8, OWN, 256),
        w_down[0],
    ).T


def solution(mesh):
    placed = (
        P(("side", "row"), "col", None),
        P(("side", "row"), None, None),
        P(("side", "row")),
        P("col", None, None),
        P("col", ("side", "row")),
        P("col", ("side", "row")),
        P(("side", "row")),
        P("col", None),
        P("col", None),
        P(("side", "row"), None, "col"),
        P(("side", "row"), None, "col"),
        P(("side", "row"), "col", None),
    )
    return jax.shard_map(
        shards, mesh=mesh, in_specs=placed, out_specs=P("col", ("side", "row")), check_vma=False
    )
```

```python
import jax
import jax.numpy as jnp
from jax import lax
from jax.experimental import pallas as pl
from jax.experimental.pallas import tpu as pltpu
from jax.sharding import PartitionSpec as P

D = 7168
ROPE = 64
HD = 128
HALF = 64
OWN = 448
PAIR = 896
MESH = pl.DeviceIdType.MESH
BF16 = jnp.bfloat16
F32 = jnp.float32

LANES = ((0, 384), (384, 256), (640, 256))
ORDERS = (
    (("x", "y", "z"), ("y", "z", "x"), ("z", "x", "y")),
    (("y", "z", "x"), ("z", "x", "y"), ("x", "y", "z")),
)
HEAD_LANES = ((0, 1152), (1152, 896))
SUM_LANES = ((0, 512), (512, 384))
LOW, HIGH, ALL = (0, 32), (32, 32), (0, 64)
DIRECT_GATHERS = ((0, 0), (1, 0), (0, 1))
DIRECT_SCATTERS = ((0, 1), (0, 2), (1, 1), (1, 2))
GROUP = 16


class Place:
    def __init__(self):
        self.side, self.row, self.col = (lax.axis_index(name) for name in ("side", "row", "col"))
        z_hi, y = lax.div(self.row, 4), lax.rem(self.row, 4)
        z_lo, x = lax.div(self.col, 4), lax.rem(self.col, 4)
        at = {"x": x, "y": y, "z": z_hi * 2 + z_lo}
        self.coord = {a: [at[a]] + [lax.rem(at[a] + k, 4) for k in (1, 2, 3)] for a in "xyz"}
        self.bits = {a: [(lax.div(j, 2), lax.rem(j, 2)) for j in self.coord[a]] for a in "xyz"}
        self.sibling = (1 - self.side, self.row, self.col)
        self.ids = {"x": [], "y": [], "z": []}
        for k in range(4):
            high, low = self.bits["z"][k]
            self.ids["x"].append((self.side, self.row, z_lo * 4 + self.coord["x"][k]))
            self.ids["y"].append((self.side, z_hi * 4 + self.coord["y"][k], self.col))
            self.ids["z"].append((self.side, high * 4 + y, low * 4 + x))

    def view(self, ref, at, rows, lanes, lead=()):
        index = [slice(None)] * 6
        if "x" in at:
            index[1], index[2] = self.bits["x"][at["x"]]
        if "y" in at:
            index[4], index[5] = self.bits["y"][at["y"]]
        if "z" in at:
            index[3], index[0] = self.bits["z"][at["z"]]
        return ref.at[(*lead, *index, pl.ds(*rows), pl.ds(*lanes))]


def remote(src, dst, send_sem, recv_sem, device):
    return pltpu.make_async_remote_copy(
        src_ref=src,
        dst_ref=dst,
        send_sem=send_sem,
        recv_sem=recv_sem,
        device_id=device,
        device_id_type=MESH,
    )


class RingGather:
    def __init__(self, here, axis, bundle, halves, sems):
        self.here, self.axis, self.bundle, self.halves, self.sems = here, axis, bundle, halves, sems

    def copy(self, direction, piece):
        send, recv = self.sems
        up = (1, 3)[direction]
        half = self.halves[direction if piece != 1 else 1 - direction]
        ref = self.bundle(0 if piece < 2 else 4 - up, half)
        device = self.here.ids[self.axis][up]
        return remote(ref, ref, send.at[direction, piece], recv.at[direction, piece], device)

    def start(self):
        for piece in range(2):
            for direction in range(2):
                self.copy(direction, piece).start()

    def relay(self):
        for direction in range(2):
            self.copy(direction, 0).wait_recv()
            self.copy(direction, 2).start()

    def near(self):
        for direction in range(2):
            self.copy(direction, 1).wait_recv()

    def far(self):
        for direction in range(2):
            self.copy(direction, 2).wait_recv()

    def drain(self):
        for direction in range(2):
            for piece in range(3):
                self.copy(direction, piece).wait_send()


class RingScatter:
    def __init__(self, here, axis, bundle, halves, arrived, sems):
        self.here, self.axis, self.bundle, self.halves = here, axis, bundle, halves
        self.arrived, self.sems = arrived, sems

    def place(self, direction, piece):
        k = 2 if piece == 0 else (1, 3)[direction]
        return self.bundle(k, self.halves[direction if piece != 1 else 1 - direction])

    def copy(self, direction, piece):
        send, recv = self.sems
        return remote(
            self.place(direction, piece),
            self.arrived.at[direction, piece],
            send.at[direction, piece],
            recv.at[direction, piece],
            self.here.ids[self.axis][(1, 3)[direction]],
        )

    def start(self):
        for piece in range(2):
            for direction in range(2):
                self.copy(direction, piece).start()

    def relay(self):
        for direction in range(2):
            self.copy(direction, 0).wait_recv()
            target = self.place(direction, 2)
            target[...] = (target[...].astype(F32) + self.arrived[direction, 0].astype(F32)).astype(BF16)
            self.copy(direction, 2).start()

    def finish(self, use=None):
        for direction in range(2):
            self.copy(direction, 1).wait_recv()
            self.copy(direction, 2).wait_recv()
        for rows, (first, second) in zip(self.halves, ((2, 1), (1, 2))):
            target = self.bundle(0, rows)
            value = target[...].astype(F32) + (
                self.arrived[0, first].astype(F32) + self.arrived[1, second].astype(F32)
            )
            if use is None:
                target[...] = value.astype(BF16)
            else:
                use(rows, value)

    def drain(self):
        for direction in range(2):
            for piece in range(3):
                self.copy(direction, piece).wait_send()


class DirectGather:
    def __init__(self, here, axis, bundle, halves, sems):
        self.here, self.axis, self.bundle, self.sems = here, axis, bundle, sems
        self.rows = (halves[0][0], 2 * halves[0][1])

    def copies(self):
        send, recv = self.sems
        ref = self.bundle(0, self.rows)
        for k in (2, 1, 3):
            yield remote(ref, ref, send.at[0, k - 1], recv.at[0, k - 1], self.here.ids[self.axis][k])

    def start(self):
        for copy in self.copies():
            copy.start()

    def far(self):
        for copy in self.copies():
            copy.wait_recv()

    def drain(self):
        for copy in self.copies():
            copy.wait_send()


class DirectScatter:
    def __init__(self, here, axis, bundle, halves, arrived, sems):
        self.here, self.axis, self.bundle, self.arrived, self.sems = here, axis, bundle, arrived, sems
        self.rows = (halves[0][0], 2 * halves[0][1])

    def copies(self):
        send, recv = self.sems
        for k in (2, 1, 3):
            yield remote(
                self.bundle(k, self.rows),
                self.arrived.at[k - 1],
                send.at[0, k - 1],
                recv.at[0, k - 1],
                self.here.ids[self.axis][k],
            )

    def start(self):
        for copy in self.copies():
            copy.start()

    def finish(self, use=None):
        for copy in self.copies():
            copy.wait_recv()
        target = self.bundle(0, self.rows)
        value = target[...].astype(F32) + (
            self.arrived[0].astype(F32) + (self.arrived[1].astype(F32) + self.arrived[2].astype(F32))
        )
        if use is None:
            target[...] = value.astype(BF16)
        else:
            use(self.rows, value)

    def drain(self):
        for copy in self.copies():
            copy.wait_send()


def layer_kernel(
    head_ref, residual_ref, gain_ref, ids_ref, vals_ref, out_hbm, gate_hbm, up_hbm, down_hbm, out_ref,
    heads, proj, part_sums, z_early, z_late, x_early, x_late, pair, pair_sib, pair_all, hidden, square,
    rows_buf, weights, down, down_pairs, total, acts, squares, inverses, gates, columns,
    from_sibling, mixed, mixed_sib,
    load_sems, head_sems, flip_sems, sum_sems, pair_sems, proj_sems, head_share_sems, small_send, small_recv,
    send_sems, recv_sems, share_send, share_recv, back_send, back_recv, last_sems, *arrivals,
):
    here = Place()
    side, row, col, sibling = here.side, here.row, here.col, here.sibling
    (z_hi, z_lo), (x_hi, x_lo), (y_hi, y_lo) = (here.bits[axis][0] for axis in "zxy")
    x = here.coord["x"][0]
    far_z = here.ids["z"][2]
    flip_z = (side, row, lax.rem(col + 4, 8))

    def row_peer(k):
        return (side, lax.rem(row + k, 8), col)

    def col_peer(k):
        return (side, row, lax.rem(col + k, 8))


    loads = [
        pltpu.make_async_copy(
            source.at[core],
            weights.at[:, core, :, pl.ds(which * 256, 256)],
            load_sems.at[which * 2 + core],
        )
        for which, source in enumerate((gate_hbm, up_hbm))
        for core in range(2)
    ]
    load_proj = pltpu.make_async_copy(out_hbm, proj.at[side], load_sems.at[4])
    load_down = pltpu.make_async_copy(down_hbm, down, load_sems.at[5])
    heads[side, z_hi, y_hi, y_lo] = head_ref[...]

    barrier = pltpu.get_barrier_semaphore()
    peers = [sibling, *map(row_peer, range(1, 8)), *map(col_peer, range(1, 8)), here.ids["z"][1], here.ids["z"][3]]
    for peer in peers:
        pl.semaphore_signal(barrier, inc=1, device_id=peer, device_id_type=MESH)
    pl.semaphore_wait(barrier, len(peers))

    def head_view(which, at, rows):
        return heads.at[(side, *at, pl.ds(*rows), pl.ds(*HEAD_LANES[which]))]

    def head_ring(index, which, z):
        return RingGather(
            here,
            "y",
            lambda k, rows: head_view(which, (z, *here.bits["y"][k]), rows),
            (LOW, HIGH),
            (head_sems.at[0, index], head_sems.at[1, index]),
        )

    def head_flip(index, which, k):
        ref = head_view(which, (z_hi, *here.bits["y"][k]), ALL)
        return remote(ref, ref, flip_sems.at[0, index], flip_sems.at[1, index], far_z)

    flips = [head_flip(0, 0, 0)] + [head_flip(1 + k, 1, k) for k in range(4)]
    rings = [head_ring(0, 1, z_hi), head_ring(1, 0, z_hi), head_ring(2, 0, 1 - z_hi)]
    flips[0].start()
    rings[0].start()
    rings[1].start()
    flips[1].start()
    load_proj.start()
    for load in loads:
        load.start()
    load_down.start()

    owner = side * 8 + row
    chosen = jnp.where(ids_ref[...] == owner, vals_ref[...], 0.0)
    gates[col] = jnp.broadcast_to(jnp.sum(chosen, axis=0, keepdims=True), (8, 128))
    square[0:OWN] = residual_ref[...].astype(F32)
    square[OWN:512] = jnp.zeros((512 - OWN, 128), F32)
    residual = square[...].T.astype(BF16)
    for half in range(2):
        pair[half, 0:HALF] = residual[half * HALF : (half + 1) * HALF, 0:OWN]
        pair[half, HALF:80] = jnp.broadcast_to(gain_ref[...].astype(F32)[None, :], (16, OWN)).astype(BF16)
    pair_copy = remote(pair.at[1 - side], pair_sib, pair_sems.at[0], pair_sems.at[1], sibling)
    pair_copy.start()
    proj_copy = remote(out_hbm, proj.at[side], proj_sems.at[0], proj_sems.at[1], sibling)
    proj_copy.start()
    def smalls(kind, ref, name):
        @pl.loop(0, 7)
        def _(k):
            peer = row_peer(k + 1) if kind == 1 else col_peer(k + 1)
            getattr(remote(ref, ref, small_send.at[kind, k], small_recv.at[kind, k], peer), name)()

    smalls(0, gates.at[col], "start")

    rings[0].relay()
    flips[0].wait_recv()
    rings[2].start()
    rings[0].near()
    flips[2].start()
    flips[4].start()
    rings[1].relay()
    rings[0].far()
    flips[3].start()
    head_shares = []
    for index, (which, z) in enumerate(((1, z_hi), (0, z_hi), (0, 1 - z_hi), (1, 1 - z_hi))):
        ref = head_view(which, (z, slice(None), 1 - side), ALL)
        head_shares.append(remote(ref, ref, head_share_sems.at[0, index], head_share_sems.at[1, index], sibling))
    head_shares[0].start()

    pair_copy.wait_recv()

    @pl.when(side == 0)
    def _():
        pair_all[:, 0:OWN] = pair[0]
        pair_all[:, OWN:PAIR] = pair_sib[...]

    @pl.when(side == 1)
    def _():
        pair_all[:, 0:OWN] = pair_sib[...]
        pair_all[:, OWN:PAIR] = pair[1]

    rings[2].relay()
    for ring, share_now in ((rings[1], head_shares[1]), (rings[2], head_shares[2])):
        ring.near()
        ring.far()
        share_now.start()
    for flip in flips[1:]:
        flip.wait_recv()
    head_shares[3].start()

    load_proj.wait()
    proj_copy.wait_recv()

    def project(source):
        lhs = heads[source, :, :, side].reshape(4 * HALF, 2048)
        value = lax.dot_general(
            lhs, proj[...].reshape(PAIR, 2048), (((1,), (1,)), ((), ())), preferred_element_type=F32
        )
        part_sums[source] = value.astype(BF16).reshape(4, HALF, PAIR)


    def x_ring(kind, index, which, lead, arrived):
        return kind(
            here,
            "x",
            lambda k, rows: part_sums.at[lead, here.coord["x"][k], pl.ds(*rows), pl.ds(*SUM_LANES[which])],
            (LOW, HIGH),
            arrived,
            (sum_sems.at[0, index], sum_sems.at[1, index]),
        )

    early_flip = remote(
        part_sums.at[1 - z_lo, :, :, pl.ds(*SUM_LANES[1])], z_early, flip_sems.at[0, 5], flip_sems.at[1, 5], flip_z
    )
    first_ring = x_ring(RingScatter, 0, 0, side, x_early.at[0])
    second_ring = x_ring(RingScatter, 2, 0, 1 - side, x_early.at[1])
    project(side)
    first_ring.start()
    for copy in head_shares:
        copy.wait_recv()
    project(1 - side)
    early_flip.start()
    second_ring.start()
    first_ring.relay()
    second_ring.relay()
    early_flip.wait_recv()
    mine = part_sums.at[z_lo, :, :, pl.ds(*SUM_LANES[1])]
    mine[...] = (mine[...].astype(F32) + z_early[...].astype(F32)).astype(BF16)
    late_ring = x_ring(DirectScatter, 1, 1, z_lo, x_late)
    late_ring.start()
    first_ring.finish()
    second_ring.finish()
    late_flip = remote(
        part_sums.at[1 - z_lo, x, :, pl.ds(*SUM_LANES[0])], z_late, flip_sems.at[0, 6], flip_sems.at[1, 6], flip_z
    )
    late_flip.start()
    late_flip.wait_recv()
    left = pl.ds(*SUM_LANES[0])
    hidden[:, left] = pair_all[0:HALF, left].astype(F32) + (
        part_sums[z_lo, x, :, left].astype(F32) + z_late[...].astype(F32)
    )

    def right(rows, value):
        spot = (pl.ds(*rows), pl.ds(*SUM_LANES[1]))
        hidden[spot] = pair_all[spot].astype(F32) + value

    late_ring.finish(right)
    rows_buf[side, z_lo, x_hi, x_lo, z_hi, y_hi, y_lo] = (
        hidden[...] * pair_all[HALF : HALF + 1].astype(F32)
    ).astype(BF16)

    def per_core(step):
        for core in range(2):

            @pl.when(side == core)
            def _(core=core):
                step(ORDERS[core])

    def halves(t):
        return (t * 32, 16), (t * 32 + 16, 16)

    def gather_rings(t, phase, orders):
        for part in range(3):
            axis = orders[part][phase]
            own = {a: 0 for a in orders[part][phase:]}
            yield (DirectGather if (t, phase) in DIRECT_GATHERS else RingGather)(
                here,
                axis,
                lambda k, rows, part=part, own=own, axis=axis: here.view(
                    rows_buf, {**own, axis: k}, rows, LANES[part], (side,)
                ),
                halves(t),
                (send_sems.at[0, t, part, phase], recv_sems.at[0, t, part, phase]),
            )

    def scatter_rings(t, phase, orders):
        for part in range(3):
            axis = orders[part][phase]
            done = {a: 0 for a in orders[part][:phase]}
            yield (DirectScatter if (t, phase) in DIRECT_SCATTERS else RingScatter)(
                here,
                axis,
                lambda k, rows, part=part, done=done, axis=axis: here.view(
                    rows_buf, {**done, axis: k}, rows, LANES[part], (side,)
                ),
                halves(t),
                arrivals[(t * 3 + phase) * 3 + part],
                (send_sems.at[1, t, part, phase], recv_sems.at[1, t, part, phase]),
            )

    def each(rings, *names):
        def step(orders):
            made = list(rings(orders))
            for name in names:
                for ring in made:
                    getattr(ring, name)()

        per_core(step)

    def gather(t, phase, *names):
        each(lambda orders: gather_rings(t, phase, orders), *names)

    def scatter(t, phase, *names):
        each(lambda orders: scatter_rings(t, phase, orders), *names)

    def share(t, part, k, orders):
        ref = here.view(rows_buf, {orders[part][2]: k}, (t * 32, 32), LANES[part], (side,))
        return remote(ref, ref, share_send.at[t, part, k], share_recv.at[t, part, k], sibling)

    def shares(t, steps, name):
        def step(orders):
            for part in range(3):
                for k in steps:
                    getattr(share(t, part, k, orders), name)()

        per_core(step)

    def chunk(r):
        return lax.div(r, 4), lax.rem(lax.div(r, 2), 2), lax.rem(r, 2)

    def back(t, r):
        return remote(
            rows_buf.at[(1 - side,) + (slice(None),) * 3 + chunk(r) + (pl.ds(t * 32, 32),)],
            from_sibling.at[t, r],
            back_send.at[t, r],
            back_recv.at[t, r],
            sibling,
        )

    def experts(t, half, place):
        total[...] = jnp.zeros_like(total)

        @pl.loop(0, 8)
        def _(r):
            lhs = rows_buf[(half,) + (slice(None),) * 3 + chunk(r) + (pl.ds(t * 32, 32),)].reshape(256, PAIR)
            total[...] += jnp.dot(lhs, weights[r].reshape(PAIR, 512), preferred_element_type=F32)

        gate_rows = columns[pl.ds(pl.multiple_of(half * HALF + t * 32, 32), 32)]
        for c in range(8):
            first = c * 32
            scale = columns[t * 32 : t * 32 + 32, place + c : place + c + 1]
            gate_part = total[first : first + 32, :256] * scale
            up_part = total[first : first + 32, 256:] * (scale * gate_rows[:, c : c + 1])
            acts[half, first : first + 32] = (gate_part / (1.0 + jnp.exp(-gate_part)) * up_part).astype(BF16)

    def down_theirs(t):
        @pl.loop(0, 8)
        def _(r):
            value = jnp.dot(acts[1 - side], down_pairs[r], preferred_element_type=F32).astype(BF16)
            rows_buf[(1 - side,) + (slice(None),) * 3 + chunk(r) + (pl.ds(t * 32, 32),)] = value.reshape(2, 2, 2, 32, PAIR)
            back(t, r).start()

    def down_own(t):
        @pl.loop(0, 8)
        def _(r):
            value = jnp.dot(acts[side], down_pairs[r], preferred_element_type=F32)
            back(t, r).wait_recv()
            value = value + from_sibling[t, r].reshape(256, PAIR).astype(F32)
            rows_buf[(side,) + (slice(None),) * 3 + chunk(r) + (pl.ds(t * 32, 32),)] = value.astype(BF16).reshape(
                2, 2, 2, 32, PAIR
            )

    def final(t):
        def step(orders):
            for part, ring in enumerate(scatter_rings(t, 2, orders)):

                def use(rows, value, part=part):
                    spot = (pl.ds(*rows), pl.ds(*LANES[part]))
                    mixed[spot] = (hidden[spot] + value).astype(BF16)

                ring.finish(use)

        per_core(step)

    def experts_own(t):
        experts(t, side, 8)

    def experts_theirs(t):
        experts(t, 1 - side, 16)

    def last(t):
        rows = pl.ds(t * 32, 32)
        return remote(mixed.at[rows], mixed_sib.at[rows], last_sems.at[0, t], last_sems.at[1, t], sibling)

    gather(0, 0, "start")
    gather(1, 0, "start")
    value = hidden[...]
    columns[0:HALF] = jnp.broadcast_to(jnp.sum(value * value, axis=1, keepdims=True), (HALF, 128))
    columns[HALF:128] = jnp.zeros((HALF, 128), F32)
    squares[row] = columns[...].T[0:8]
    smalls(1, squares.at[row], "start")
    gather(0, 0, "far")
    gather(0, 1, "start")
    gather(1, 0, "far")
    gather(1, 1, "start")
    smalls(1, squares.at[row], "wait_recv")
    inverses[side, col] = lax.rsqrt(jnp.sum(squares[...], axis=0) / D + 1e-06)
    smalls(2, inverses.at[side, col], "start")
    gather(0, 1, "far")
    gather(0, 2, "start")
    shares(0, (0,), "start")
    gather(1, 1, "relay")
    gather(1, 1, "near", "far")
    smalls(2, inverses.at[side, col], "wait_recv")
    inverse_share = remote(
        inverses.at[side], inverses.at[side], pair_sems.at[4], pair_sems.at[5], sibling
    )
    inverse_share.start()
    load_down.wait()
    for r in range(8):
        for core in range(2):
            down_pairs[r, :, core * OWN : (core + 1) * OWN] = down[
                :, (core * 8 + r) * OWN : (core * 8 + r + 1) * OWN
            ]
    smalls(0, gates.at[col], "wait_recv")
    inverse_share.wait_recv()
    columns[...] = jnp.zeros_like(columns)
    for c in range(8):
        columns[c : c + 1] = gates[c, 0:1]
        columns[8 + c : 9 + c] = inverses[side, c, 0:1]
        columns[16 + c : 17 + c] = inverses[1 - side, c, 0:1]
    columns[...] = columns[...].T
    for load in loads:
        load.wait()
    gather(0, 2, "relay")
    gather(0, 2, "near")
    shares(0, (1, 3), "start")
    gather(0, 2, "far")
    gather(1, 2, "start")
    shares(0, (2,), "start")
    shares(1, (0,), "start")
    experts_own(0)
    shares(0, (0, 1, 2, 3), "wait_recv")
    experts_theirs(0)
    down_theirs(0)
    gather(1, 2, "relay")
    for phase in range(3):
        gather(0, phase, "drain")
    shares(0, (0, 1, 2, 3), "wait_send")
    gather(1, 2, "near")
    shares(1, (1, 3), "start")
    down_own(0)
    gather(1, 2, "far")
    shares(1, (2,), "start")
    scatter(0, 0, "start")
    experts_own(1)
    shares(1, (0, 1, 2, 3), "wait_recv")
    experts_theirs(1)
    down_theirs(1)
    scatter(0, 0, "relay")
    for phase in range(3):
        gather(1, phase, "drain")
    shares(1, (0, 1, 2, 3), "wait_send")
    down_own(1)
    scatter(1, 0, "start")
    scatter(0, 0, "finish")
    scatter(0, 1, "start")
    scatter(1, 0, "relay")
    scatter(0, 1, "finish")
    scatter(0, 2, "start")
    final(0)
    last(0).start()
    scatter(1, 0, "finish")
    scatter(1, 1, "start")
    scatter(1, 1, "finish")
    scatter(1, 2, "start")
    final(1)
    last(1).start()
    for t in range(2):
        last(t).wait_recv()

    def transposed(top, bottom):
        square[0:PAIR // 2, 0:HALF] = top.astype(F32).T
        square[0:PAIR // 2, HALF:128] = bottom.astype(F32).T
        out_ref[...] = square[0:OWN].astype(BF16)

    @pl.when(side == 0)
    def _():
        transposed(mixed[:, 0:OWN], mixed_sib[:, 0:OWN])

    @pl.when(side == 1)
    def _():
        transposed(mixed_sib[:, OWN:PAIR], mixed[:, OWN:PAIR])

    for t in range(2):
        last(t).wait_send()
    for ring in (*rings, first_ring, second_ring, late_ring):
        ring.drain()
    for copy in (
        *flips, *head_shares, early_flip, late_flip, pair_copy, proj_copy, inverse_share,
    ):
        copy.wait_send()
    smalls(0, gates.at[col], "wait_send")
    smalls(1, squares.at[row], "wait_send")
    smalls(2, inverses.at[side, col], "wait_send")
    for t in range(2):
        for phase in range(3):
            scatter(t, phase, "drain")

        @pl.loop(0, 8)
        def _(r, t=t):
            back(t, r).wait_send()


ARRIVALS = [
    (
        *((3,) if (t, phase) in DIRECT_SCATTERS else (2, 3)),
        *(2,) * (4 - 2 * phase),
        32 if (t, phase) in DIRECT_SCATTERS else 16,
        LANES[part][1],
    )
    for t in range(2)
    for phase in range(3)
    for part in range(3)
]

VMEM = pl.BlockSpec(memory_space=pltpu.VMEM)
ANY = pl.BlockSpec(memory_space=pl.ANY)
DMA = pltpu.SemaphoreType.DMA


def attend_kernel(
    lengths_ref, queries_hbm, cache_hbm, up_hbm, out_ref, queries, cache, up, latent, query_sems, cache_sems, up_sem
):
    def loads(group):
        rows = pl.ds(group * GROUP, GROUP)
        return (
            pltpu.make_async_copy(queries_hbm.at[rows], queries.at[rows], query_sems.at[group]),
            pltpu.make_async_copy(cache_hbm.at[rows], cache.at[rows], cache_sems.at[group]),
        )

    for group in range(HALF // GROUP):
        for load in loads(group):
            load.start()
    load_up = pltpu.make_async_copy(up_hbm, up, up_sem)
    load_up.start()
    lane = lax.broadcasted_iota(jnp.int32, (16, 128), 1)

    @pl.loop(0, HALF // GROUP)
    def _(group):
        for load in loads(group):
            load.wait()
        scores = []
        for i in range(GROUP):
            r = group * GROUP + i
            score = jnp.dot(queries[r], cache[r], preferred_element_type=F32) * (HD + ROPE) ** (-0.5)
            scores.append(jnp.where(lane < lengths_ref[r], score, -jnp.inf))
        scores = jnp.concatenate(scores, axis=0)
        terms = jnp.exp(scores - jnp.max(scores, axis=1, keepdims=True))
        probs = (terms / jnp.sum(terms, axis=1, keepdims=True)).astype(BF16)
        for i in range(GROUP):
            r = group * GROUP + i
            value = lax.dot_general(
                probs[i * 16 : (i + 1) * 16],
                cache[r, 0:512],
                (((1,), (1,)), ((), ())),
                preferred_element_type=F32,
            )
            for k in range(4):
                latent[k, pl.ds(pl.multiple_of(r * 16, 16), 16)] = value[:, k * 128 : k * 128 + 128]

    load_up.wait()
    for head in range(16):
        rows = jnp.concatenate([latent[k, pl.ds(head, HALF, stride=16)] for k in range(4)], axis=1).astype(BF16)
        out_ref[:, head * HD : (head + 1) * HD] = jnp.dot(
            rows, up[head], preferred_element_type=F32
        ).astype(BF16)


def attend_call(lengths, queries, cache, w_uv):
    return pl.pallas_call(
        attend_kernel,
        out_shape=jax.ShapeDtypeStruct((HALF, 16 * HD), BF16),
        in_specs=[pl.BlockSpec(memory_space=pltpu.SMEM), ANY, ANY, ANY],
        out_specs=VMEM,
        scratch_shapes=[
            pltpu.VMEM((HALF, 16, 576), BF16),
            pltpu.VMEM((HALF, 576, 128), BF16),
            pltpu.VMEM((16, 512, HD), BF16),
            pltpu.VMEM((4, HALF * 16, 128), F32),
            pltpu.SemaphoreType.DMA((HALF // GROUP,)),
            pltpu.SemaphoreType.DMA((HALF // GROUP,)),
            pltpu.SemaphoreType.DMA,
        ],
        compiler_params=pltpu.CompilerParams(vmem_limit_bytes=58 * 2**20),
        cost_estimate=pl.CostEstimate(
            flops=2 * 64 * 16 * 128 * 1700, bytes_accessed=14 * 2**20, transcendentals=2**17
        ),
    )(lengths, queries, cache, w_uv)


def layer_call(*args):
    scratch = [
        pltpu.VMEM((2, 2, 2, 2, HALF, 2048), BF16),
        pltpu.VMEM((2, OWN, 2048), BF16),
        pltpu.VMEM((2, 4, HALF, PAIR), BF16),
        pltpu.VMEM((4, HALF, SUM_LANES[1][1]), BF16),
        pltpu.VMEM((HALF, SUM_LANES[0][1]), BF16),
        pltpu.VMEM((2, 2, 3, 32, SUM_LANES[0][1]), BF16),
        pltpu.VMEM((3, HALF, SUM_LANES[1][1]), BF16),
        pltpu.VMEM((2, 80, OWN), BF16),
        pltpu.VMEM((80, OWN), BF16),
        pltpu.VMEM((80, PAIR), BF16),
        pltpu.VMEM((HALF, PAIR), F32),
        pltpu.VMEM((512, 128), F32),
        pltpu.VMEM((2, 2, 2, 2, 2, 2, 2, HALF, PAIR), BF16),
        pltpu.VMEM((8, 2, OWN, 512), BF16),
        pltpu.VMEM((256, D), BF16),
        pltpu.VMEM((8, 256, PAIR), BF16),
        pltpu.VMEM((256, 512), F32),
        pltpu.VMEM((2, 256, 256), BF16),
        pltpu.VMEM((8, 8, 128), F32),
        pltpu.VMEM((2, 8, 8, 128), F32),
        pltpu.VMEM((8, 8, 128), F32),
        pltpu.VMEM((128, 128), F32),
        pltpu.VMEM((2, 8, 2, 2, 2, 32, PAIR), BF16),
        pltpu.VMEM((HALF, PAIR), BF16),
        pltpu.VMEM((HALF, PAIR), BF16),
        DMA((6,)),
        DMA((2, 3, 2, 3)),
        DMA((2, 7)),
        DMA((2, 3, 2, 3)),
        DMA((8,)),
        DMA((2,)),
        DMA((2, 4)),
        DMA((3, 7)),
        DMA((3, 7)),
        DMA((2, 2, 3, 3, 2, 3)),
        DMA((2, 2, 3, 3, 2, 3)),
        DMA((2, 3, 4)),
        DMA((2, 3, 4)),
        DMA((2, 8)),
        DMA((2, 8)),
        DMA((2, 2)),
        *[pltpu.VMEM(shape, BF16) for shape in ARRIVALS],
    ]
    return pl.pallas_call(
        layer_kernel,
        out_shape=jax.ShapeDtypeStruct((OWN, 2 * HALF), BF16),
        in_specs=[VMEM] * 5 + [ANY] * 4,
        out_specs=VMEM,
        scratch_shapes=scratch,
        compiler_params=pltpu.CompilerParams(
            collective_id=0, has_side_effects=True, vmem_limit_bytes=58 * 2**20
        ),
        cost_estimate=pl.CostEstimate(
            flops=2 * 1024 * 7168 * 1000, bytes_accessed=16 * 2**20, transcendentals=2**18
        ),
    )(*args)


def shards(
    queries,
    cache,
    lengths,
    w_uv,
    w_out,
    residual_in,
    norm_gain,
    expert_ids,
    gate_vals,
    w_gate,
    w_up,
    w_down,
):
    head_out = attend_call(lengths, queries, cache.swapaxes(1, 2), w_uv)
    return layer_call(
        head_out,
        residual_in.T,
        norm_gain,
        expert_ids.T,
        gate_vals.T,
        w_out.T,
        w_gate.reshape(2, 8, OWN, 256),
        w_up.reshape(2, 8, OWN, 256),
        w_down[0],
    ).T


def solution(mesh):
    placed = (
        P(("side", "row"), "col", None),
        P(("side", "row"), None, None),
        P(("side", "row")),
        P("col", None, None),
        P("col", ("side", "row")),
        P("col", ("side", "row")),
        P(("side", "row")),
        P("col", None),
        P("col", None),
        P(("side", "row"), None, "col"),
        P(("side", "row"), None, "col"),
        P(("side", "row"), "col", None),
    )
    return jax.shard_map(
        shards, mesh=mesh, in_specs=placed, out_specs=P("col", ("side", "row")), check_vma=False
    )
```
